32 devices in a mesh: vel: 4 (over y, core), sx: 4 (over z), sy: 2 (over x).
Axes of the slice: x: 2, y: 2, z: 4, core: 2. Of those that a mesh axis runs over, the one named last changes fastest.
Arguments:
- scaled_population_table: float32 [32, 16, 32768], P('sx', 'sy', 'vel'), may hold values from 0 to 8, as said below
Outputs:
- advanced: float32 [32, 16, 32768], P('sx', 'sy', 'vel')
The draws below stay inside these ranges and needn't reach their ends.
Inputs may be any that keep to these rules, and one draw needn't show every extreme that they name: `scaled_population_table`: every entry is positive.
All inputs are finite; a program needn't handle non-finite values.
Results may differ from the reference program's by a relative error of at most 0.0003.
Values sent between devices are 32-bit elements; how exact they have to be, the bound alone decides.
No kernel may reach another device: no remote copies, remote signals or barrier semaphores. Data moves between devices by JAX's collectives and lax.ppermute only.
A program may use at most 64 MiB of HBM per device.

```python
import math
import jax
import jax.numpy as jnp
from jax import lax

KV = 32
NV = 32768
GRID_ROWS_X = 32
GRID_ROWS_Y = 16


def draw_scaled_population_table(key, part):
    subkeys = jax.random.split(jax.random.fold_in(key, 17), 3)
    vel_index = jnp.arange(NV, dtype=jnp.int32)
    levels = (vel_index // (KV * KV), vel_index // KV % KV, vel_index % KV)
    particle_speeds = [(2 * one_level + 1 - KV).astype(jnp.float32) * (4.5 / KV) for one_level in levels]

    def population(subkey):
        sampler_seed_handle = jax.random.split(subkey, 3)
        local_matter_amount = jax.random.uniform(sampler_seed_handle[0], (GRID_ROWS_X, GRID_ROWS_Y, 1), minval=0.3, maxval=1.2)
        bulk_flow_components = jax.random.uniform(sampler_seed_handle[1], (3, GRID_ROWS_X, GRID_ROWS_Y, 1), minval=-0.8, maxval=0.8)
        kinetic_warmth_level = jnp.exp(jax.random.uniform(sampler_seed_handle[2], (GRID_ROWS_X, GRID_ROWS_Y, 1), minval=math.log(0.6), maxval=math.log(1.8)))
        velocity_dispersion_width = (particle_speeds[0] - bulk_flow_components[0]) ** 2 + (particle_speeds[1] - bulk_flow_components[1]) ** 2 + (particle_speeds[2] - bulk_flow_components[2]) ** 2
        return local_matter_amount * kinetic_warmth_level ** (-1.5) * jnp.exp(-velocity_dispersion_width / (2.0 * kinetic_warmth_level))
    mixture = population(subkeys[0]) + population(subkeys[1])
    jitter = jax.random.uniform(subkeys[2], (GRID_ROWS_X, GRID_ROWS_Y, NV), minval=-0.25, maxval=0.25)
    return (mixture * (1.0 + jitter)).astype(jnp.float32)


def setup_inputs(seed: int = 0) -> dict:
    keys = jax.random.split(jax.random.key(seed), 2)
    scaled_population_table = draw_scaled_population_table(jax.random.fold_in(keys[1], 71), 0)
    return dict(scaled_population_table=scaled_population_table)


vel_bound = 4.5
time_step = 0.25 / 4.5
baseline_collision_interval = 0.25
power_law_index = 0.81
diffusivity_ratio_coefficient = 2.0 / 3.0
highest = lax.Precision.HIGHEST


def velocity_table(vel_index):
    levels = (vel_index // (KV * KV), (vel_index // KV) % KV, vel_index % KV)
    return tuple((2 * one_level + 1 - KV).astype(jnp.float32) * (vel_bound / KV) for one_level in levels)


def quad_weight():
    return (2.0 * vel_bound / KV) ** 3 * (2.0 * math.pi) ** -1.5


def minmod(former, latter):
    return 0.5 * (jnp.sign(former) + jnp.sign(latter)) * jnp.minimum(jnp.abs(former), jnp.abs(latter))


def flux_change(padded, velocity, along_axis):
    length = padded.shape[along_axis]
    behind = lax.slice_in_dim(padded, 0, length - 2, axis=along_axis)
    middle = lax.slice_in_dim(padded, 1, length - 1, axis=along_axis)
    ahead_cell = lax.slice_in_dim(padded, 2, length, axis=along_axis)
    slopes = minmod(middle - behind, ahead_cell - middle)
    face_low = lax.slice_in_dim(middle + 0.5 * slopes, 0, length - 3, axis=along_axis)
    face_high = lax.slice_in_dim(middle - 0.5 * slopes, 1, length - 2, axis=along_axis)
    fluxes = jnp.maximum(velocity, 0.0) * face_low + jnp.minimum(velocity, 0.0) * face_high
    return lax.slice_in_dim(fluxes, 1, length - 3, axis=along_axis) - lax.slice_in_dim(fluxes, 0, length - 4, axis=along_axis)


def block_width():
    return math.gcd(NV, 2048)


def block_speeds(block_index):
    block_start = (block_index * block_width()).astype(jnp.int32)
    vel_index = block_start + jnp.arange(block_width(), dtype=jnp.int32)
    return block_start, velocity_table(vel_index)


def local_fluid_snapshot(scaled_population_table):
    blocks = NV // block_width()

    def add_bulk(block_index, running):
        block_start, particle_speeds = block_speeds(block_index)
        vel_piece = lax.dynamic_slice_in_dim(scaled_population_table, block_start, block_width(), 2)
        squares = particle_speeds[0] * particle_speeds[0] + particle_speeds[1] * particle_speeds[1] + particle_speeds[2] * particle_speeds[2]
        moment_basis = jnp.stack([jnp.ones_like(particle_speeds[0]), particle_speeds[0], particle_speeds[1], particle_speeds[2], squares])
        return running + jnp.einsum("xyv,mv->xym", vel_piece, moment_basis, precision=highest)

    integrated_sums_list = lax.fori_loop(0, blocks, add_bulk, jnp.zeros((GRID_ROWS_X, GRID_ROWS_Y, 5), jnp.float32)) * quad_weight()
    local_matter_amount = integrated_sums_list[..., 0:1]
    bulk_flow_components = tuple(integrated_sums_list[..., column:column + 1] / local_matter_amount for column in (1, 2, 3))
    bulk_flow_norm_square = bulk_flow_components[0] * bulk_flow_components[0] + bulk_flow_components[1] * bulk_flow_components[1] + bulk_flow_components[2] * bulk_flow_components[2]
    kinetic_warmth_level = (integrated_sums_list[..., 4:5] / local_matter_amount - bulk_flow_norm_square) / 3.0

    def add_heat(block_index, running):
        block_start, particle_speeds = block_speeds(block_index)
        vel_piece = lax.dynamic_slice_in_dim(scaled_population_table, block_start, block_width(), 2)
        neighbour_displacement_list = [particle_speeds[column] - bulk_flow_components[column] for column in range(3)]
        velocity_dispersion_width = neighbour_displacement_list[0] * neighbour_displacement_list[0] + neighbour_displacement_list[1] * neighbour_displacement_list[1] + neighbour_displacement_list[2] * neighbour_displacement_list[2]
        weighted = vel_piece * velocity_dispersion_width
        return running + jnp.stack([jnp.sum(weighted * neighbour_displacement_list[column], axis=2) for column in range(3)], axis=-1)

    heat_total = lax.fori_loop(0, blocks, add_heat, jnp.zeros((GRID_ROWS_X, GRID_ROWS_Y, 3), jnp.float32)) * (0.5 * quad_weight())
    energy_current_triple = tuple(heat_total[..., column:column + 1] for column in range(3))
    return local_matter_amount, bulk_flow_components, kinetic_warmth_level, energy_current_triple


def advance(scaled_population_table):
    local_matter_amount, bulk_flow_components, kinetic_warmth_level, energy_current_triple = local_fluid_snapshot(scaled_population_table)
    collision_rate_coefficient = local_matter_amount * kinetic_warmth_level ** (1.0 - power_law_index) / baseline_collision_interval

    def one_block(block_index):
        block_start, particle_speeds = block_speeds(block_index)
        vel_piece = lax.dynamic_slice_in_dim(scaled_population_table, block_start, block_width(), 2)
        padded = jnp.pad(vel_piece, ((2, 2), (2, 2), (0, 0)), mode="wrap")
        neighbour_displacement_list = [particle_speeds[column] - bulk_flow_components[column] for column in range(3)]
        velocity_dispersion_width = neighbour_displacement_list[0] * neighbour_displacement_list[0] + neighbour_displacement_list[1] * neighbour_displacement_list[1] + neighbour_displacement_list[2] * neighbour_displacement_list[2]
        gaussian_rest_profile = local_matter_amount * kinetic_warmth_level ** -1.5 * jnp.exp(-velocity_dispersion_width / (2.0 * kinetic_warmth_level))
        directional_energy_current = neighbour_displacement_list[0] * energy_current_triple[0] + neighbour_displacement_list[1] * energy_current_triple[1] + neighbour_displacement_list[2] * energy_current_triple[2]
        shakhov_attractor_profile = gaussian_rest_profile * (1.0 + (1.0 - diffusivity_ratio_coefficient) * directional_energy_current / (5.0 * local_matter_amount * kinetic_warmth_level * kinetic_warmth_level) * (velocity_dispersion_width / kinetic_warmth_level - 5.0))
        transport = flux_change(padded[:, 2:-2], particle_speeds[0], 0) + flux_change(padded[2:-2, :], particle_speeds[1], 1)
        return vel_piece + time_step * (collision_rate_coefficient * (shakhov_attractor_profile - vel_piece) - transport)

    stacked = lax.map(one_block, jnp.arange(NV // block_width(), dtype=jnp.int32))
    return jnp.moveaxis(stacked, 0, 2).reshape(GRID_ROWS_X, GRID_ROWS_Y, NV)


def reference(scaled_population_table):
    sectioned = advance(scaled_population_table)
    return 0.5 * scaled_population_table + 0.5 * advance(sectioned)
```

```python
import functools
import math

import jax
import jax.numpy as jnp
from jax import lax
from jax.experimental import pallas as pl
from jax.experimental.pallas import tpu as pltpu
from jax.sharding import PartitionSpec as P

KV = 32
CHUNKS = 1
LANES = 128
ROWS = 8

vel_bound = 4.5
time_step = 0.25 / 4.5
collision_interval = 0.25
power_law_index = 0.81
diffusivity_ratio = 2.0 / 3.0
step = vel_bound / KV
weight = (2.0 * vel_bound / KV) ** 3 * (2.0 * math.pi) ** (-1.5)
f32 = jnp.float32

TILES = KV * KV // LANES
HALF = TILES // 2
PER_TILE = LANES // KV
SLOTS = LANES // ROWS


def limited(p, q):
    return jnp.maximum(jnp.minimum(p, jnp.maximum(q, 0.0)), jnp.minimum(q, 0.0))


def lane_index():
    return lax.broadcasted_iota(jnp.int32, (ROWS, LANES), 1)


def component(digit):
    return (2 * digit + 1 - KV).astype(f32) * step


def lane_components(tile):
    lane = lane_index()
    return component(tile * PER_TILE + lane // KV), component(lane % KV)


def changes(cells):
    out = []
    slope = cells[1] - cells[0]
    face = None
    for k in range(1, len(cells) - 1):
        ahead = cells[k + 1] - cells[k]
        new_face = cells[k] + 0.5 * limited(slope, ahead)
        if face is not None:
            out.append(new_face - face)
        slope, face = ahead, new_face
    return out


def send_x(source, tile, flow, primary, secondary):
    last = jnp.where(flow, 7, 0)
    before = jnp.where(flow, 6, 1)
    first = jnp.where(flow, 0, 7)
    row = lambda x: pl.ds(pl.multiple_of(x * ROWS, ROWS), ROWS)
    primary[tile, 0] = source[tile, row(before), :]
    primary[tile, 1] = source[tile, row(last), :]
    secondary[tile] = source[tile, row(first), :]


def send_y(source, pair, low, high, across):
    column = lambda tile, y: source[tile, pl.ds(y, ROWS, stride=ROWS), :]
    across[0, pair, 0] = column(high, 6)
    across[0, pair, 1] = column(high, 7)
    across[0, pair, 2] = column(low, 7)
    across[1, pair, 0] = column(low, 1)
    across[1, pair, 1] = column(low, 0)
    across[1, pair, 2] = column(high, 0)


def flow_of(vel_size, vel_name):
    return lax.axis_index(vel_name) >= vel_size // 2


def pack_kernel(vel_size, levels, table, cells, primary, secondary, across):
    flow = flow_of(vel_size, "vel")

    def one(i, carry):
        level, quarter = i // HALF, i % HALF
        low = level * TILES + quarter
        high = low + HALF
        for tile in (low, high):
            lanes = pl.ds(pl.multiple_of(tile * LANES, LANES), LANES)
            for x in range(ROWS):
                cells[tile, x * ROWS : (x + 1) * ROWS, :] = table[x, :, lanes]
            send_x(cells, tile, flow, primary, secondary)
        send_y(cells, i, low, high, across)
        return carry

    lax.fori_loop(0, levels * HALF, one, 0)


def sums_kernel(levels, all_levels, first_level, cells, *rest):
    sums = rest[-1]
    lane = lane_index()
    base = lax.axis_index("vel") * all_levels + first_level
    speed = [component(base + level) for level in range(levels)]

    def one(x, total):
        acc = [jnp.zeros((ROWS, LANES), f32) for _ in range(13)]
        row = pl.ds(pl.multiple_of(x * ROWS, ROWS), ROWS)
        for tile in range(TILES):
            cb, ce = lane_components(tile)
            m0 = m1 = m2 = m3 = None
            for level in range(levels):
                g = cells[level * TILES + tile, row, :]
                g1 = g * speed[level]
                g2 = g1 * speed[level]
                g3 = g2 * speed[level]
                if level == 0:
                    m0, m1, m2, m3 = g, g1, g2, g3
                else:
                    m0, m1, m2, m3 = m0 + g, m1 + g1, m2 + g2, m3 + g3
            square = cb * cb + ce * ce
            b0 = cb * m0
            e0 = ce * m0
            terms = (
                m0, m1, b0, e0, m2, cb * b0, ce * e0, cb * m1, ce * m1, cb * e0,
                m3 + square * m1, cb * m2 + square * b0, ce * m2 + square * e0,
            )
            acc = [a + t for a, t in zip(acc, terms)]
        for m in range(13):
            total = jnp.where(lane == x * SLOTS + m, jnp.sum(acc[m], axis=1, keepdims=True), total)
        return total

    total = lax.fori_loop(0, ROWS, one, jnp.zeros((ROWS, LANES), f32))
    for other in rest[:-1]:
        total = total + other[...]
    sums[...] = total


def tables(parts, levels, base, scale, tab_b, tab_a, keep):
    sums = parts[0][...]
    for part in parts[1:]:
        sums = sums + part[...]
    sums = sums * weight
    for x in range(ROWS):
        m = [
            jnp.broadcast_to(sums[:, x * SLOTS + i : x * SLOTS + i + 1], (ROWS, LANES))
            for i in range(13)
        ]
        n = m[0]
        inverse = 1.0 / n
        u = [m[i] * inverse for i in (1, 2, 3)]
        uu = u[0] * u[0] + u[1] * u[1] + u[2] * u[2]
        energy = m[4] + m[5] + m[6]
        temp = (energy * inverse - uu) * (1.0 / 3.0)
        rows = ((4, 7, 8), (7, 5, 9), (8, 9, 6))
        q = []
        for i in range(3):
            r = rows[i]
            stress = m[r[0]] * u[0] + m[r[1]] * u[1] + m[r[2]] * u[2]
            q.append(0.5 * (m[10 + i] - 2.0 * stress - u[i] * energy + 2.0 * n * u[i] * uu))
        log_temp = jnp.log(temp)
        rate = n * jnp.exp((1.0 - power_law_index) * log_temp) * (time_step / collision_interval)
        cold = 1.0 / temp
        half_cold = 0.5 * cold
        size = scale * rate * n * (cold * lax.rsqrt(temp))
        lift = (1.0 - diffusivity_ratio) / (5.0 * n * temp * temp)
        keep[x] = scale * (1.0 - rate)
        ql = [part * lift for part in q]
        for tile in range(TILES):
            cb, ce = lane_components(tile)
            db, de = cb - u[1], ce - u[2]
            square = db * db + de * de
            tab_b[x, tile, 0] = size * jnp.exp(-square * half_cold)
            tab_b[x, tile, 1] = db * ql[1] + de * ql[2]
            tab_b[x, tile, 2] = square * cold - 5.0
        for level in range(levels):
            da = component(base + level) - u[0]
            square = da * da
            tab_a[x, level, 0] = jnp.exp(-square * half_cold)
            tab_a[x, level, 1] = da * ql[0]
            tab_a[x, level, 2] = square * cold


def update_kernel(vel_size, levels, all_levels, first_level, parts_count, last, *refs):
    cells, from_x, from_x2, from_y = refs[:4]
    parts = refs[4 : 4 + parts_count]
    refs = refs[4 + parts_count :]
    if last:
        table, out, tab_b, tab_a, keep, side = refs
    else:
        out, primary, secondary, across, tab_b, tab_a, keep, side = refs
    scale = 0.5 if last else 1.0
    flow = flow_of(vel_size, "vel")
    base = lax.axis_index("vel") * all_levels + first_level
    tables(parts, levels, base, scale, tab_b, tab_a, keep)
    lane = lane_index()
    xs = [jnp.where(flow, k, ROWS - 1 - k) for k in range(ROWS)]

    def one(i, carry):
        level, quarter = i // HALF, i % HALF
        a_speed = jnp.abs(component(base + level)) * (time_step * scale)
        b_digit = quarter * PER_TILE + lane // KV
        for sign in (0, 1):
            sub = quarter + sign * HALF
            tile = level * TILES + sub
            b_speed = jnp.abs(component(b_digit + sign * (KV // 2))) * (time_step * scale)
            ys = range(ROWS) if sign else range(ROWS - 1, -1, -1)
            line = [from_y[1 - sign, i, 0], from_y[1 - sign, i, 1]]
            line += [cells[tile, pl.ds(y, ROWS, stride=ROWS), :] for y in ys]
            line += [from_y[sign, i, 2]]
            for y, change in zip(ys, changes(line)):
                side[sign, pl.ds(y, ROWS, stride=ROWS), :] = b_speed * change
            rows = [pl.ds(pl.multiple_of(x * ROWS, ROWS), ROWS) for x in xs]
            line = [from_x[tile, 0], from_x[tile, 1]]
            line += [cells[tile, row, :] for row in rows]
            line += [from_x2[tile]]
            for k, change in enumerate(changes(line)):
                x, row = xs[k], rows[k]
                source = tab_a[x, level, 0] * tab_b[x, sub, 0]
                bend = tab_a[x, level, 1] + tab_b[x, sub, 1]
                wide = tab_a[x, level, 2] + tab_b[x, sub, 2]
                new = line[k + 2] * keep[x] + (source + source * (bend * wide))
                new = new - (a_speed * change + side[sign, row, :])
                if last:
                    lanes = pl.ds(pl.multiple_of(tile * LANES, LANES), LANES)
                    out[x, :, lanes] = 0.5 * table[x, :, lanes] + new
                else:
                    out[tile, row, :] = new
            if not last:
                send_x(out, tile, flow, primary, secondary)
        if not last:
            low = level * TILES + quarter
            send_y(out, i, low, low + HALF, across)
        return carry

    lax.fori_loop(0, levels * HALF, one, 0)


def local(sizes, table):
    vel_size, sx_size, sy_size = sizes
    cells_x, cells_y, count = table.shape
    all_levels = count // (KV * KV)
    chunks = math.gcd(CHUNKS, all_levels)
    levels = all_levels // chunks
    assert cells_x == ROWS and cells_y == ROWS and vel_size % 2 == 0
    assert count == all_levels * KV * KV
    width = count // chunks
    tiles = levels * TILES
    shape = jax.ShapeDtypeStruct
    cells_shape = shape((tiles, ROWS * ROWS, LANES), f32)
    primary_shape = shape((tiles, 2, ROWS, LANES), f32)
    secondary_shape = shape((tiles, ROWS, LANES), f32)
    across_shape = shape((2, levels * HALF, 3, ROWS, LANES), f32)
    sums_shape = shape((ROWS, LANES), f32)
    message_shapes = (cells_shape, primary_shape, secondary_shape, across_shape)
    whole = pl.BlockSpec(memory_space=pltpu.VMEM)
    params = pltpu.CompilerParams(vmem_limit_bytes=40 * 1024 * 1024)
    half = vel_size // 2

    def along_x(array, sign):
        pairs = []
        for v in range(vel_size):
            way = sign if v >= half else -sign
            pairs += [(v * sx_size + i, v * sx_size + (i + way) % sx_size) for i in range(sx_size)]
        return lax.ppermute(array, ("vel", "sx"), pairs)

    def along_y(array):
        if sy_size == 2:
            return lax.ppermute(array, "sy", [(0, 1), (1, 0)])
        up = [(i, (i + 1) % sy_size) for i in range(sy_size)]
        down = [(j, i) for i, j in up]
        return jnp.stack([lax.ppermute(array[0], "sy", up), lax.ppermute(array[1], "sy", down)])

    def exchange(messages):
        primary, secondary, across = messages
        return along_x(primary, 1), along_x(secondary, -1), along_y(across)

    def gathered(sums):
        if vel_size > 4:
            return (lax.psum(sums, "vel"),)
        others = [
            lax.ppermute(sums, "vel", [(i, (i + k) % vel_size) for i in range(vel_size)])
            for k in range(1, vel_size)
        ]
        return (sums, *others)

    def piece(c):
        return pl.BlockSpec((ROWS, ROWS, width), lambda i, c=c: (0, 0, c))

    def pack(c):
        return pl.pallas_call(
            functools.partial(pack_kernel, vel_size, levels),
            grid=(1,),
            out_shape=message_shapes,
            in_specs=[piece(c)],
            out_specs=[whole] * 4,
            compiler_params=params,
            name="pack",
        )(table)

    def sums_of(c, cells, *earlier):
        return pl.pallas_call(
            functools.partial(sums_kernel, levels, all_levels, c * levels),
            out_shape=sums_shape,
            in_specs=[whole] * (1 + len(earlier)),
            out_specs=whole,
            compiler_params=params,
            name="sums",
        )(cells, *earlier)

    scratch = [
        pltpu.VMEM((ROWS, TILES, 3, ROWS, LANES), f32),
        pltpu.VMEM((ROWS, levels, 3, ROWS, LANES), f32),
        pltpu.VMEM((ROWS, ROWS, LANES), f32),
        pltpu.VMEM((2, ROWS * ROWS, LANES), f32),
    ]

    def advance(c, cells, messages, parts):
        return pl.pallas_call(
            functools.partial(
                update_kernel, vel_size, levels, all_levels, c * levels, len(parts), False
            ),
            out_shape=message_shapes,
            in_specs=[whole] * (4 + len(parts)),
            out_specs=[whole] * 4,
            scratch_shapes=scratch,
            compiler_params=params,
            name="advance",
        )(cells, *messages, *parts)

    def finish(c, cells, messages, parts):
        return pl.pallas_call(
            functools.partial(
                update_kernel, vel_size, levels, all_levels, c * levels, len(parts), True
            ),
            grid=(1,),
            out_shape=shape((ROWS, ROWS, width), f32),
            in_specs=[whole] * (4 + len(parts)) + [piece(c)],
            out_specs=whole,
            scratch_shapes=scratch,
            compiler_params=params,
            name="finish",
        )(cells, *messages, *parts, table)

    def all_sums(pieces):
        sums = ()
        for c, cells in enumerate(pieces):
            sums = (sums_of(c, cells, *sums),)
        return gathered(sums[0])

    packed = [pack(c) for c in range(chunks)]
    arrived = [exchange(p[1:]) for p in packed]
    parts = all_sums([p[0] for p in packed])
    staged = [advance(c, packed[c][0], arrived[c], parts) for c in range(chunks)]
    arrived = [exchange(s[1:]) for s in staged]
    parts = all_sums([s[0] for s in staged])
    done = [finish(c, staged[c][0], arrived[c], parts) for c in range(chunks)]
    return done[0] if chunks == 1 else jnp.concatenate(done, axis=2)


def solution(mesh):
    sizes = tuple(mesh.shape[name] for name in ("vel", "sx", "sy"))
    return jax.shard_map(
        functools.partial(local, sizes),
        mesh=mesh,
        in_specs=(P("sx", "sy", "vel"),),
        out_specs=P("sx", "sy", "vel"),
        check_vma=False,
    )
```

```python
import functools
import math

import jax
import jax.numpy as jnp
from jax import lax
from jax.experimental import pallas as pl
from jax.experimental.pallas import tpu as pltpu
from jax.sharding import PartitionSpec as P

KV = 32
LANES = 128
ROWS = 8

vel_bound = 4.5
time_step = 0.25 / 4.5
collision_interval = 0.25
power_law_index = 0.81
diffusivity_ratio = 2.0 / 3.0
step = vel_bound / KV
weight = (2.0 * vel_bound / KV) ** 3 * (2.0 * math.pi) ** (-1.5)
f32 = jnp.float32

TILES = KV * KV // LANES
HALF = TILES // 2
PER_TILE = LANES // KV
SLOTS = LANES // ROWS


def limited(p, q):
    return jnp.maximum(jnp.minimum(p, jnp.maximum(q, 0.0)), jnp.minimum(q, 0.0))


def lane_index():
    return lax.broadcasted_iota(jnp.int32, (ROWS, LANES), 1)


def component(digit):
    return (2 * digit + 1 - KV).astype(f32) * step


def lane_components(tile):
    lane = lane_index()
    return component(tile * PER_TILE + lane // KV), component(lane % KV)


def flow_of(vel_size):
    return lax.axis_index("vel") >= vel_size // 2


def order_of(flow):
    return [jnp.where(flow, k, ROWS - 1 - k) for k in range(ROWS)]


def row_of(x):
    return pl.ds(pl.multiple_of(x * ROWS, ROWS), ROWS)


def column_of(y):
    return pl.ds(y, ROWS, stride=ROWS)


def lanes_of(tile):
    return pl.ds(pl.multiple_of(tile * LANES, LANES), LANES)


def columns_in_order(sign):
    return range(ROWS) if sign else range(ROWS - 1, -1, -1)


def inner_changes(cells):
    slopes = [cells[k + 1] - cells[k] for k in range(ROWS - 1)]
    faces = [cells[k] + 0.5 * limited(slopes[k - 1], slopes[k]) for k in range(1, ROWS - 1)]
    middle = [faces[k] - faces[k - 1] for k in range(1, ROWS - 2)]
    return [faces[0], *middle, -faces[-1]]


def outer_changes(far, near, p0, p1, p6, p7, ahead):
    slope = p0 - near
    entry = near + 0.5 * limited(near - far, slope)
    first = p0 + 0.5 * limited(slope, p1 - p0)
    leave = p7 + 0.5 * limited(p7 - p6, ahead - p7)
    return first - entry, -first, leave


def pack_x_kernel(vel_size, table, primary, secondary, sems):
    flow = flow_of(vel_size)
    xs = order_of(flow)
    copies = [
        pltpu.make_async_copy(table.at[xs[6]], primary.at[0], sems.at[0]),
        pltpu.make_async_copy(table.at[xs[7]], primary.at[1], sems.at[1]),
        pltpu.make_async_copy(table.at[xs[0]], secondary.at[0], sems.at[2]),
    ]
    for copy in copies:
        copy.start()
    for copy in copies:
        copy.wait()


def send_y(source, pair, low, high, up, down):
    up[pair, 0] = source[high, column_of(6), :]
    up[pair, 1] = source[high, column_of(7), :]
    up[pair, 2] = source[low, column_of(7), :]
    down[pair, 0] = source[low, column_of(1), :]
    down[pair, 1] = source[low, column_of(0), :]
    down[pair, 2] = source[high, column_of(0), :]


def pack_y_kernel(levels, table, cells, up, down, held, sems):
    width = TILES * LANES

    def copy(level):
        lanes = pl.ds(pl.multiple_of(level * width, width), width)
        return pltpu.make_async_copy(table.at[:, :, lanes], held.at[level], sems.at[level])

    for level in range(levels):
        copy(level).start()

    def one(level, carry):
        copy(level).wait()
        for quarter in range(HALF):
            low = level * TILES + quarter
            high = low + HALF
            for tile, sub in ((low, quarter), (high, quarter + HALF)):
                for x in range(ROWS):
                    cells[tile, x * ROWS : (x + 1) * ROWS, :] = held[
                        level, x, :, sub * LANES : (sub + 1) * LANES
                    ]
            send_y(cells, level * HALF + quarter, low, high, up, down)
        return carry

    lax.fori_loop(0, levels, one, 0)


def sums_kernel(levels, cells, sums):
    lane = lane_index()
    base = lax.axis_index("vel") * levels
    speed = [component(base + level) for level in range(levels)]

    def one(x, total):
        acc = [jnp.zeros((ROWS, LANES), f32) for _ in range(13)]
        row = row_of(x)
        for tile in range(TILES):
            cb, ce = lane_components(tile)
            m0 = m1 = m2 = m3 = None
            for level in range(levels):
                g = cells[level * TILES + tile, row, :]
                g1 = g * speed[level]
                g2 = g1 * speed[level]
                g3 = g2 * speed[level]
                if level == 0:
                    m0, m1, m2, m3 = g, g1, g2, g3
                else:
                    m0, m1, m2, m3 = m0 + g, m1 + g1, m2 + g2, m3 + g3
            square = cb * cb + ce * ce
            b0 = cb * m0
            e0 = ce * m0
            terms = (
                m0, m1, b0, e0, m2, cb * b0, ce * e0, cb * m1, ce * m1, cb * e0,
                m3 + square * m1, cb * m2 + square * b0, ce * m2 + square * e0,
            )
            acc = [a + t for a, t in zip(acc, terms)]
        for m in range(13):
            total = jnp.where(lane == x * SLOTS + m, jnp.sum(acc[m], axis=1, keepdims=True), total)
        return total

    sums[...] = lax.fori_loop(0, ROWS, one, jnp.zeros((ROWS, LANES), f32))


def tables(parts, levels, base, scale, tab_b, tab_a, keep):
    sums = parts[0][...]
    for part in parts[1:]:
        sums = sums + part[...]
    sums = sums * weight
    for x in range(ROWS):
        m = [
            jnp.broadcast_to(sums[:, x * SLOTS + i : x * SLOTS + i + 1], (ROWS, LANES))
            for i in range(13)
        ]
        n = m[0]
        inverse = 1.0 / n
        u = [m[i] * inverse for i in (1, 2, 3)]
        uu = u[0] * u[0] + u[1] * u[1] + u[2] * u[2]
        energy = m[4] + m[5] + m[6]
        temp = (energy * inverse - uu) * (1.0 / 3.0)
        rows = ((4, 7, 8), (7, 5, 9), (8, 9, 6))
        q = []
        for i in range(3):
            r = rows[i]
            stress = m[r[0]] * u[0] + m[r[1]] * u[1] + m[r[2]] * u[2]
            q.append(0.5 * (m[10 + i] - 2.0 * stress - u[i] * energy + 2.0 * n * u[i] * uu))
        log_temp = jnp.log(temp)
        rate = n * jnp.exp((1.0 - power_law_index) * log_temp) * (time_step / collision_interval)
        cold = 1.0 / temp
        half_cold = 0.5 * cold
        size = scale * rate * n * (cold * lax.rsqrt(temp))
        lift = (1.0 - diffusivity_ratio) / (5.0 * n * temp * temp)
        keep[x] = scale * (1.0 - rate)
        ql = [part * lift for part in q]
        for tile in range(TILES):
            cb, ce = lane_components(tile)
            db, de = cb - u[1], ce - u[2]
            square = db * db + de * de
            tab_b[x, tile, 0] = size * jnp.exp(-square * half_cold)
            tab_b[x, tile, 1] = db * ql[1] + de * ql[2]
            tab_b[x, tile, 2] = square * cold - 5.0
        for level in range(levels):
            da = component(base + level) - u[0]
            square = da * da
            tab_a[x, level, 0] = jnp.exp(-square * half_cold)
            tab_a[x, level, 1] = da * ql[0]
            tab_a[x, level, 2] = square * cold


def speeds(base, level, quarter, sign, scale):
    b_digit = quarter * PER_TILE + lane_index() // KV + sign * (KV // 2)
    a_speed = jnp.abs(component(base + level)) * (time_step * scale)
    return a_speed, jnp.abs(component(b_digit)) * (time_step * scale)


def local_kernel(vel_size, levels, last, *refs):
    cells, parts, first, (out, tab_b, tab_a, keep, side) = refs[0], refs[1:2], refs[2:-5], refs[-5:]
    scale = 0.5 if last else 1.0
    base = lax.axis_index("vel") * levels
    tables(parts, levels, base, scale, tab_b, tab_a, keep)
    xs = order_of(flow_of(vel_size))
    rows = [row_of(x) for x in xs]
    for sign in (0, 1):
        side[sign] = jnp.zeros((ROWS * ROWS, LANES), f32)

    def one(i, carry):
        level, quarter = i // HALF, i % HALF
        for sign in (0, 1):
            sub = quarter + sign * HALF
            tile = level * TILES + sub
            a_speed, b_speed = speeds(base, level, quarter, sign, scale)
            ys = columns_in_order(sign)
            line = [cells[tile, column_of(y), :] for y in ys]
            for k, change in enumerate(inner_changes(line)):
                side[sign, column_of(ys[k + 1]), :] = b_speed * change
            line = [cells[tile, row, :] for row in rows]
            changes = inner_changes(line)
            for k in range(ROWS):
                x, row = xs[k], rows[k]
                source = tab_a[x, level, 0] * tab_b[x, sub, 0]
                bend = tab_a[x, level, 1] + tab_b[x, sub, 1]
                wide = tab_a[x, level, 2] + tab_b[x, sub, 2]
                new = line[k] * keep[x] + (source + source * (bend * wide))
                moved = side[sign, row, :]
                if k > 0:
                    moved = moved + a_speed * changes[k - 1]
                new = new - moved
                if last:
                    new = 0.5 * first[0][tile, row, :] + new
                out[tile, row, :] = new
        return carry

    lax.fori_loop(0, levels * HALF, one, 0)


def edge_changes(cells, tile, i, sign, rows, speed, from_x, up, down):
    a_speed, b_speed = speed
    mine, other = (up, down) if sign else (down, up)
    ys = columns_in_order(sign)
    line = [cells[tile, column_of(ys[k]), :] for k in (0, 1, 6, 7)]
    across = outer_changes(mine[i, 0], mine[i, 1], *line, other[i, 2])
    line = [cells[tile, rows[k], :] for k in (0, 1, 6, 7)]
    far, near, ahead = from_x(tile)
    along = outer_changes(far, near, *line, ahead)
    return [a_speed * c for c in along], [b_speed * c for c in across]


EDGE = (0, 1, ROWS - 1)
GROUP = 1


def correct_kernel(vel_size, levels, partial, cells, from_x1, from_x2, from_up, from_down, *refs):
    out, primary, secondary, up, down = refs
    base = lax.axis_index("vel") * levels
    xs = order_of(flow_of(vel_size))
    rows = [row_of(x) for x in xs]

    def from_x(tile):
        lanes = lanes_of(tile)
        return from_x1[0, :, lanes], from_x1[1, :, lanes], from_x2[0, :, lanes]

    def one(level, carry):
        for group in range(0, HALF, GROUP):
            changes = []
            for quarter in range(group, group + GROUP):
                for sign in (0, 1):
                    tile = level * TILES + quarter + sign * HALF
                    along, across = edge_changes(
                        cells, tile, level * HALF + quarter, sign, rows,
                        speeds(base, level, quarter, sign, 1.0), from_x, from_up, from_down,
                    )
                    changes.append((tile, columns_in_order(sign), along, across))
            old = [[out[t, column_of(ys[k]), :] for k in EDGE] for t, ys, _, _ in changes]
            for (t, ys, _, across), before in zip(changes, old):
                for k, value, change in zip(EDGE, before, across):
                    out[t, column_of(ys[k]), :] = value - change
            old = [[out[t, rows[k], :] for k in EDGE] for t, _, _, _ in changes]
            for (t, _, along, _), before in zip(changes, old):
                new = [value - change for value, change in zip(before, along)]
                for k, value in zip(EDGE, new):
                    out[t, rows[k], :] = value
                secondary[t] = new[0]
                primary[t, 1] = new[2]
            for t, _, _, _ in changes:
                primary[t, 0] = out[t, rows[6], :]
            for quarter in range(group, group + GROUP):
                low = level * TILES + quarter
                send_y(out, level * HALF + quarter, low, low + HALF, up, down)
        return carry

    lax.fori_loop(0, levels, one, 0)


def finish_kernel(vel_size, levels, partial, cells, from_x1, from_x2, from_up, from_down, *refs):
    result, held, side, sems = refs
    base = lax.axis_index("vel") * levels
    xs = order_of(flow_of(vel_size))
    rows = [row_of(x) for x in xs]
    width = TILES * LANES
    for sub in range(TILES):
        side[sub] = jnp.zeros((ROWS * ROWS, LANES), f32)

    def from_x(tile):
        return from_x1[tile, 0], from_x1[tile, 1], from_x2[tile]

    def copy(level):
        lanes = pl.ds(pl.multiple_of(level * width, width), width)
        return pltpu.make_async_copy(held.at[level], result.at[:, :, lanes], sems.at[level])

    def one(level, carry):
        for quarter in range(HALF):
            for sign in (0, 1):
                sub = quarter + sign * HALF
                tile = level * TILES + sub
                ys = columns_in_order(sign)
                along, across = edge_changes(
                    cells, tile, level * HALF + quarter, sign, rows,
                    speeds(base, level, quarter, sign, 0.5), from_x, from_up, from_down,
                )
                for k, change in zip(EDGE, across):
                    side[sub, column_of(ys[k]), :] = change
                extra = dict(zip(EDGE, along))
                for k in range(ROWS):
                    new = partial[tile, rows[k], :] - side[sub, rows[k], :]
                    if k in extra:
                        new = new - extra[k]
                    held[level, xs[k], :, sub * LANES : (sub + 1) * LANES] = new
        copy(level).start()
        return carry

    lax.fori_loop(0, levels, one, 0)
    for level in range(levels):
        copy(level).wait()


def local(sizes, table):
    vel_size, sx_size, sy_size = sizes
    cells_x, cells_y, count = table.shape
    levels = count // (KV * KV)
    assert cells_x == ROWS and cells_y == ROWS and vel_size % 2 == 0
    assert count == levels * KV * KV
    tiles = levels * TILES
    shape = lambda *dims: jax.ShapeDtypeStruct(dims, f32)
    cells_shape = shape(tiles, ROWS * ROWS, LANES)
    across_shape = shape(levels * HALF, 3, ROWS, LANES)
    whole = pl.BlockSpec(memory_space=pltpu.VMEM)
    outside = pl.BlockSpec(memory_space=pltpu.HBM)
    half = vel_size // 2

    def call(kernel, name, ins, outs, *args, scratch=(), aliases={}, static=(), room=16):
        specs = [outside if a is table else whole for a in args]
        return pl.pallas_call(
            functools.partial(kernel, *static),
            out_shape=outs,
            in_specs=specs,
            out_specs=ins,
            scratch_shapes=list(scratch),
            input_output_aliases=aliases,
            compiler_params=pltpu.CompilerParams(vmem_limit_bytes=room * 1024 * 1024),
            name=name,
        )(*args)

    def along_x(array, sign):
        pairs = []
        for v in range(vel_size):
            way = sign if v >= half else -sign
            pairs += [(v * sx_size + i, v * sx_size + (i + way) % sx_size) for i in range(sx_size)]
        return lax.ppermute(array, ("vel", "sx"), pairs)

    def along_y(array, way):
        return lax.ppermute(array, "sy", [(i, (i + way) % sy_size) for i in range(sy_size)])

    def exchange(primary, secondary, up, down):
        return along_x(primary, 1), along_x(secondary, -1), along_y(up, 1), along_y(down, -1)

    def gathered(sums):
        if vel_size & (vel_size - 1):
            return lax.psum(sums, "vel")
        d = 1
        while d < vel_size:
            sums = sums + lax.ppermute(sums, "vel", [(i, i ^ d) for i in range(vel_size)])
            d *= 2
        return sums

    def sums_of(cells):
        return gathered(
            call(sums_kernel, "sums", whole, shape(ROWS, LANES), cells, static=(levels,))
        )

    table_scratch = [
        pltpu.VMEM((ROWS, TILES, 3, ROWS, LANES), f32),
        pltpu.VMEM((ROWS, levels, 3, ROWS, LANES), f32),
        pltpu.VMEM((ROWS, ROWS, LANES), f32),
        pltpu.VMEM((2, ROWS * ROWS, LANES), f32),
    ]
    held = pltpu.VMEM((levels, ROWS, ROWS, TILES * LANES), f32)

    primary, secondary = call(
        pack_x_kernel, "pack_x", [whole] * 2,
        (shape(2, ROWS, count), shape(1, ROWS, count)),
        table, scratch=[pltpu.SemaphoreType.DMA((3,))], static=(vel_size,),
    )
    cells, up, down = call(
        pack_y_kernel, "pack_y", [whole] * 3, (cells_shape, across_shape, across_shape),
        table, scratch=[held, pltpu.SemaphoreType.DMA((levels,))], static=(levels,),
    )
    arrived = exchange(primary, secondary, up, down)
    partial = call(
        local_kernel, "local", whole, cells_shape, cells, sums_of(cells),
        scratch=table_scratch, static=(vel_size, levels, False),
    )
    sectioned, *messages = call(
        correct_kernel, "correct", [whole] * 5,
        (cells_shape, shape(tiles, 2, ROWS, LANES), shape(tiles, ROWS, LANES), across_shape, across_shape),
        partial, cells, *arrived, static=(vel_size, levels), aliases={0: 0},
    )
    arrived = exchange(*messages)
    partial = call(
        local_kernel, "local", whole, cells_shape, sectioned, sums_of(sectioned), cells,
        scratch=table_scratch, static=(vel_size, levels, True),
    )
    return call(
        finish_kernel, "finish", outside, shape(*table.shape), partial, sectioned, *arrived,
        scratch=[
            held,
            pltpu.VMEM((TILES, ROWS * ROWS, LANES), f32),
            pltpu.SemaphoreType.DMA((levels,)),
        ],
        static=(vel_size, levels),
    )


def solution(mesh):
    sizes = tuple(mesh.shape[name] for name in ("vel", "sx", "sy"))
    return jax.shard_map(
        functools.partial(local, sizes),
        mesh=mesh,
        in_specs=(P("sx", "sy", "vel"),),
        out_specs=P("sx", "sy", "vel"),
        check_vma=False,
    )
```

```python
import functools
import math

import jax
import jax.numpy as jnp
from jax import lax
from jax.experimental import pallas as pl
from jax.experimental.pallas import tpu as pltpu
from jax.sharding import PartitionSpec as P

KV = 32
SPLIT = (1, 2)
PARTED = ()
LANES = 128
ROWS = 8

vel_bound = 4.5
time_step = 0.25 / 4.5
collision_interval = 0.25
power_law_index = 0.81
diffusivity_ratio = 2.0 / 3.0
step = vel_bound / KV
weight = (2.0 * vel_bound / KV) ** 3 * (2.0 * math.pi) ** (-1.5)
f32 = jnp.float32

TILES = KV * KV // LANES
HALF = TILES // 2
PER_TILE = LANES // KV
SLOTS = LANES // ROWS


def limited(p, q):
    return jnp.maximum(jnp.minimum(p, jnp.maximum(q, 0.0)), jnp.minimum(q, 0.0))


def lane_index():
    return lax.broadcasted_iota(jnp.int32, (ROWS, LANES), 1)


def component(digit):
    return (2 * digit + 1 - KV).astype(f32) * step


def lane_components(tile):
    lane = lane_index()
    return component(tile * PER_TILE + lane // KV), component(lane % KV)


def flow_of(vel_size):
    return lax.axis_index("vel") >= vel_size // 2


def order_of(flow):
    return [jnp.where(flow, k, ROWS - 1 - k) for k in range(ROWS)]


def row_of(x):
    return pl.ds(pl.multiple_of(x * ROWS, ROWS), ROWS)


def column_of(y):
    return pl.ds(y, ROWS, stride=ROWS)


def lanes_of(tile):
    return pl.ds(pl.multiple_of(tile * LANES, LANES), LANES)


def columns_in_order(sign):
    return range(ROWS) if sign else range(ROWS - 1, -1, -1)


def inner_changes(cells):
    slopes = [cells[k + 1] - cells[k] for k in range(ROWS - 1)]
    faces = [cells[k] + 0.5 * limited(slopes[k - 1], slopes[k]) for k in range(1, ROWS - 1)]
    middle = [faces[k] - faces[k - 1] for k in range(1, ROWS - 2)]
    return [faces[0], *middle, -faces[-1]]


def outer_changes(far, near, p0, p1, p6, p7, ahead):
    slope = p0 - near
    entry = near + 0.5 * limited(near - far, slope)
    first = p0 + 0.5 * limited(slope, p1 - p0)
    leave = p7 + 0.5 * limited(p7 - p6, ahead - p7)
    return first - entry, -first, leave


def send_y(source, pair, low, high, across):
    across[0][pair, 0] = source[high, column_of(6), :]
    across[0][pair, 1] = source[high, column_of(7), :]
    across[0][pair, 2] = source[low, column_of(7), :]
    across[1][pair, 0] = source[low, column_of(1), :]
    across[1][pair, 1] = source[low, column_of(0), :]
    across[1][pair, 2] = source[high, column_of(0), :]


def pack_kernel(vel_size, levels, bounds, table, cells, *refs):
    chunks = len(bounds)
    across, primary, secondary = refs[:chunks], refs[chunks : 2 * chunks], refs[2 * chunks]
    held, sems = refs[-2], refs[-1]
    rows = [row_of(x) for x in order_of(flow_of(vel_size))]
    width = TILES * LANES

    def copy(level):
        lanes = pl.ds(pl.multiple_of(level * width, width), width)
        return pltpu.make_async_copy(table.at[:, :, lanes], held.at[level], sems.at[level])

    for level in range(levels):
        copy(level).start()
    for c, (begin, end) in enumerate(bounds):

        def one(level, carry, c=c, begin=begin):
            copy(level).wait()
            for quarter in range(HALF):
                low = level * TILES + quarter
                high = low + HALF
                for tile, sub in ((low, quarter), (high, quarter + HALF)):
                    for x in range(ROWS):
                        cells[tile, x * ROWS : (x + 1) * ROWS, :] = held[
                            level, x, :, sub * LANES : (sub + 1) * LANES
                        ]
                    primary[c][tile - begin * TILES, 0] = cells[tile, rows[6], :]
                    primary[c][tile - begin * TILES, 1] = cells[tile, rows[7], :]
                    secondary[tile] = cells[tile, rows[0], :]
                send_y(cells, (level - begin) * HALF + quarter, low, high, halves(across[c : c + 1]))
            return carry

        lax.fori_loop(begin, end, one, 0)


def halves(refs):
    return refs if len(refs) == 2 else [refs[0].at[0], refs[0].at[1]]


def sums_kernel(levels, cells, *refs):
    sums = refs[-1]
    lane = lane_index()
    base = lax.axis_index("vel") * levels
    speed = [component(base + level) for level in range(levels)]

    def one(x, total):
        acc = [jnp.zeros((ROWS, LANES), f32) for _ in range(13)]
        row = row_of(x)
        for tile in range(TILES):
            cb, ce = lane_components(tile)
            m0 = m1 = m2 = m3 = None
            for level in range(levels):
                g = cells[level * TILES + tile, row, :]
                g1 = g * speed[level]
                g2 = g1 * speed[level]
                g3 = g2 * speed[level]
                if level == 0:
                    m0, m1, m2, m3 = g, g1, g2, g3
                else:
                    m0, m1, m2, m3 = m0 + g, m1 + g1, m2 + g2, m3 + g3
            square = cb * cb + ce * ce
            b0 = cb * m0
            e0 = ce * m0
            terms = (
                m0, m1, b0, e0, m2, cb * b0, ce * e0, cb * m1, ce * m1, cb * e0,
                m3 + square * m1, cb * m2 + square * b0, ce * m2 + square * e0,
            )
            acc = [a + t for a, t in zip(acc, terms)]
        for m in range(13):
            total = jnp.where(lane == x * SLOTS + m, jnp.sum(acc[m], axis=1, keepdims=True), total)
        return total

    sums[...] = lax.fori_loop(0, ROWS, one, jnp.zeros((ROWS, LANES), f32))


def tables(parts, levels, base, scale, tab_b, tab_a, keep):
    sums = None
    for part in parts:
        for i in range(part.shape[0] // ROWS):
            more = part[i * ROWS : (i + 1) * ROWS, :]
            sums = more if sums is None else sums + more
    sums = sums * weight
    for x in range(ROWS):
        m = [
            jnp.broadcast_to(sums[:, x * SLOTS + i : x * SLOTS + i + 1], (ROWS, LANES))
            for i in range(13)
        ]
        n = m[0]
        inverse = 1.0 / n
        u = [m[i] * inverse for i in (1, 2, 3)]
        uu = u[0] * u[0] + u[1] * u[1] + u[2] * u[2]
        energy = m[4] + m[5] + m[6]
        temp = (energy * inverse - uu) * (1.0 / 3.0)
        rows = ((4, 7, 8), (7, 5, 9), (8, 9, 6))
        q = []
        for i in range(3):
            r = rows[i]
            stress = m[r[0]] * u[0] + m[r[1]] * u[1] + m[r[2]] * u[2]
            q.append(0.5 * (m[10 + i] - 2.0 * stress - u[i] * energy + 2.0 * n * u[i] * uu))
        log_temp = jnp.log(temp)
        rate = n * jnp.exp((1.0 - power_law_index) * log_temp) * (time_step / collision_interval)
        cold = 1.0 / temp
        half_cold = 0.5 * cold
        size = scale * rate * n * (cold * lax.rsqrt(temp))
        lift = (1.0 - diffusivity_ratio) / (5.0 * n * temp * temp)
        keep[x] = scale * (1.0 - rate)
        ql = [part * lift for part in q]
        for tile in range(TILES):
            cb, ce = lane_components(tile)
            db, de = cb - u[1], ce - u[2]
            square = db * db + de * de
            tab_b[x, tile, 0] = size * jnp.exp(-square * half_cold)
            tab_b[x, tile, 1] = db * ql[1] + de * ql[2]
            tab_b[x, tile, 2] = square * cold - 5.0
        for level in range(levels):
            da = component(base + level) - u[0]
            square = da * da
            tab_a[x, level, 0] = jnp.exp(-square * half_cold)
            tab_a[x, level, 1] = da * ql[0]
            tab_a[x, level, 2] = square * cold


def speeds(base, level, quarter, sign, scale):
    b_digit = quarter * PER_TILE + lane_index() // KV + sign * (KV // 2)
    a_speed = jnp.abs(component(base + level)) * (time_step * scale)
    return a_speed, jnp.abs(component(b_digit)) * (time_step * scale)


def local_kernel(vel_size, levels, last, *refs):
    cells, parts, first, (out, tab_b, tab_a, keep, side) = refs[0], refs[1:2], refs[2:-5], refs[-5:]
    scale = 0.5 if last else 1.0
    base = lax.axis_index("vel") * levels
    tables(parts, levels, base, scale, tab_b, tab_a, keep)
    xs = order_of(flow_of(vel_size))
    rows = [row_of(x) for x in xs]
    for sign in (0, 1):
        side[sign] = jnp.zeros((ROWS * ROWS, LANES), f32)

    def one(i, carry):
        level, quarter = i // HALF, i % HALF
        for sign in (0, 1):
            sub = quarter + sign * HALF
            tile = level * TILES + sub
            a_speed, b_speed = speeds(base, level, quarter, sign, scale)
            ys = columns_in_order(sign)
            line = [cells[tile, column_of(y), :] for y in ys]
            for k, change in enumerate(inner_changes(line)):
                side[sign, column_of(ys[k + 1]), :] = b_speed * change
            line = [cells[tile, row, :] for row in rows]
            changes = inner_changes(line)
            for k in range(ROWS):
                x, row = xs[k], rows[k]
                source = tab_a[x, level, 0] * tab_b[x, sub, 0]
                bend = tab_a[x, level, 1] + tab_b[x, sub, 1]
                wide = tab_a[x, level, 2] + tab_b[x, sub, 2]
                new = line[k] * keep[x] + (source + source * (bend * wide))
                moved = side[sign, row, :]
                if k > 0:
                    moved = moved + a_speed * changes[k - 1]
                new = new - moved
                if last:
                    new = 0.5 * first[0][tile, row, :] + new
                out[tile, row, :] = new
        return carry

    lax.fori_loop(0, levels * HALF, one, 0)


def edge_changes(cells, tile, i, sign, rows, speed, from_x, from_y):
    a_speed, b_speed = speed
    mine, other = 1 - sign, sign
    ys = columns_in_order(sign)
    line = [cells[tile, column_of(ys[k]), :] for k in (0, 1, 6, 7)]
    across = outer_changes(from_y[mine][i, 0], from_y[mine][i, 1], *line, from_y[other][i, 2])
    line = [cells[tile, rows[k], :] for k in (0, 1, 6, 7)]
    far, near, ahead = from_x(tile)
    along = outer_changes(far, near, *line, ahead)
    return [a_speed * c for c in along], [b_speed * c for c in across]


EDGE = (0, 1, ROWS - 1)
GROUP = 1


def correct_kernel(vel_size, levels, start, stop, parted, partial, cells, from_x1, from_x2, from_y, *refs):
    across = halves(refs[-1 - parted :])
    out, primary, secondary = refs[-4 - parted : -1 - parted]
    from_y = halves([from_y])
    base = lax.axis_index("vel") * levels
    xs = order_of(flow_of(vel_size))
    rows = [row_of(x) for x in xs]

    def from_x(tile):
        here = tile - start * TILES
        return from_x1[here, 0], from_x1[here, 1], from_x2[tile]

    def one(level, carry):
        for group in range(0, HALF, GROUP):
            changes = []
            for quarter in range(group, group + GROUP):
                for sign in (0, 1):
                    tile = level * TILES + quarter + sign * HALF
                    along, sides = edge_changes(
                        cells, tile, (level - start) * HALF + quarter, sign, rows,
                        speeds(base, level, quarter, sign, 1.0), from_x, from_y,
                    )
                    changes.append((tile, columns_in_order(sign), along, sides))
            old = [[out[t, column_of(ys[k]), :] for k in EDGE] for t, ys, _, _ in changes]
            for (t, ys, _, sides), before in zip(changes, old):
                for k, value, change in zip(EDGE, before, sides):
                    out[t, column_of(ys[k]), :] = value - change
            old = [[out[t, rows[k], :] for k in EDGE] for t, _, _, _ in changes]
            for (t, _, along, _), before in zip(changes, old):
                mine = t - start * TILES
                new = [value - change for value, change in zip(before, along)]
                for k, value in zip(EDGE, new):
                    out[t, rows[k], :] = value
                secondary[t] = new[0]
                primary[mine, 1] = new[2]
            for t, _, _, _ in changes:
                primary[t - start * TILES, 0] = out[t, rows[6], :]
            for quarter in range(group, group + GROUP):
                low = level * TILES + quarter
                send_y(out, (level - start) * HALF + quarter, low, low + HALF, across)
        return carry

    lax.fori_loop(start, stop, one, 0)


def finish_kernel(vel_size, levels, start, stop, parted, partial, cells, from_x1, from_x2, *refs):
    from_y = halves(refs[: 1 + parted])
    result, held, side, sems = refs[-4:]
    base = lax.axis_index("vel") * levels
    xs = order_of(flow_of(vel_size))
    rows = [row_of(x) for x in xs]
    width = TILES * LANES
    for sub in range(TILES):
        side[sub] = jnp.zeros((ROWS * ROWS, LANES), f32)

    def from_x(tile):
        here = tile - start * TILES
        return from_x1[here, 0], from_x1[here, 1], from_x2[tile]

    def copy(level):
        lanes = pl.ds(pl.multiple_of(level * width, width), width)
        here = level - start
        return pltpu.make_async_copy(held.at[here], result.at[:, :, lanes], sems.at[here])

    def one(level, carry):
        for quarter in range(HALF):
            for sign in (0, 1):
                sub = quarter + sign * HALF
                tile = level * TILES + sub
                ys = columns_in_order(sign)
                along, across = edge_changes(
                    cells, tile, (level - start) * HALF + quarter, sign, rows,
                    speeds(base, level, quarter, sign, 0.5), from_x, from_y,
                )
                for k, change in zip(EDGE, across):
                    side[sub, column_of(ys[k]), :] = change
                extra = dict(zip(EDGE, along))
                for k in range(ROWS):
                    new = partial[tile, rows[k], :] - side[sub, rows[k], :]
                    if k in extra:
                        new = new - extra[k]
                    held[level - start, xs[k], :, sub * LANES : (sub + 1) * LANES] = new
        copy(level).start()
        return carry

    lax.fori_loop(start, stop, one, 0)
    for level in range(start, stop):
        copy(level).wait()


def local(sizes, table):
    vel_size, sx_size, sy_size = sizes
    cells_x, cells_y, count = table.shape
    levels = count // (KV * KV)
    assert cells_x == ROWS and cells_y == ROWS and vel_size % 2 == 0
    assert count == levels * KV * KV
    first_part = levels * SPLIT[0] // SPLIT[1]
    bounds = [(0, first_part), (first_part, levels)] if 0 < first_part < levels else [(0, levels)]
    chunks = len(bounds)
    tiles = levels * TILES
    shape = lambda *dims: jax.ShapeDtypeStruct(dims, f32)
    cells_shape = shape(tiles, ROWS * ROWS, LANES)
    across_shape = [shape(2, (b - a) * HALF, 3, ROWS, LANES) for a, b in bounds]
    primary_shape = [shape((b - a) * TILES, 2, ROWS, LANES) for a, b in bounds]
    secondary_shape = shape(tiles, ROWS, LANES)
    whole = pl.BlockSpec(memory_space=pltpu.VMEM)
    outside = pl.BlockSpec(memory_space=pltpu.HBM)
    half = vel_size // 2

    def call(kernel, name, ins, outs, *args, scratch=(), aliases={}, static=()):
        specs = [outside if a.shape == table.shape else whole for a in args]
        return pl.pallas_call(
            functools.partial(kernel, *static),
            out_shape=outs,
            in_specs=specs,
            out_specs=ins,
            scratch_shapes=list(scratch),
            input_output_aliases=aliases,
            compiler_params=pltpu.CompilerParams(vmem_limit_bytes=16 * 1024 * 1024),
            name=name,
        )(*args)

    def along_x(array, sign):
        pairs = []
        for v in range(vel_size):
            way = sign if v >= half else -sign
            pairs += [(v * sx_size + i, v * sx_size + (i + way) % sx_size) for i in range(sx_size)]
        return lax.ppermute(array, ("vel", "sx"), pairs)

    def along_y(arrays):
        ways = [[(i, (i + way) % sy_size) for i in range(sy_size)] for way in (1, -1)]
        if len(arrays) == 2:
            return tuple(lax.ppermute(a, "sy", way) for a, way in zip(arrays, ways))
        if sy_size == 2:
            return (lax.ppermute(arrays[0], "sy", ways[0]),)
        return (jnp.stack([lax.ppermute(arrays[0][i], "sy", ways[i]) for i in (0, 1)]),)

    def exchange(primary, secondary, across):
        behind = along_x(secondary, -1)
        return [(along_x(p, 1), behind, *along_y(a)) for p, a in zip(primary, across)]

    def sums_of(cells, *after):
        return call(sums_kernel, "sums", whole, shape(ROWS, LANES), cells, *after, static=(levels,))

    def first_sums(sums):
        if vel_size > 4:
            return lax.psum(sums, "vel")
        return lax.all_gather(sums, "vel", axis=0, tiled=True)

    def second_sums(sums):
        if vel_size & (vel_size - 1):
            return lax.psum(sums, "vel")
        d = 1
        while d < vel_size:
            sums = sums + lax.ppermute(sums, "vel", [(i, i ^ d) for i in range(vel_size)])
            d *= 2
        return sums

    table_scratch = [
        pltpu.VMEM((ROWS, TILES, 3, ROWS, LANES), f32),
        pltpu.VMEM((ROWS, levels, 3, ROWS, LANES), f32),
        pltpu.VMEM((ROWS, ROWS, LANES), f32),
        pltpu.VMEM((2, ROWS * ROWS, LANES), f32),
    ]
    held = lambda count: pltpu.VMEM((count, ROWS, ROWS, TILES * LANES), f32)
    copies = lambda count: pltpu.SemaphoreType.DMA((count,))

    cells, *messages, secondary = call(
        pack_kernel, "pack", [whole] * (2 * chunks + 2),
        [cells_shape] + across_shape + primary_shape + [secondary_shape],
        table, scratch=[held(levels), copies(levels)], static=(vel_size, levels, bounds),
    )
    arrived = exchange(messages[chunks:], secondary, [(m,) for m in messages[:chunks]])
    sectioned = call(
        local_kernel, "local", whole, cells_shape, cells, first_sums(sums_of(cells)),
        scratch=table_scratch, static=(vel_size, levels, False),
    )
    primary, across, partly = [], [], ()
    for c, (begin, end) in enumerate(bounds):
        parted = int(c in PARTED)
        one_way = shape((end - begin) * HALF, 3, ROWS, LANES)
        sectioned, first, secondary, *sides = call(
            correct_kernel, "correct", [whole] * (4 + parted),
            [cells_shape, primary_shape[c], secondary_shape]
            + ([one_way] * 2 if parted else [across_shape[c]]),
            sectioned, cells, *arrived[c], *partly,
            static=(vel_size, levels, begin, end, parted),
            aliases={0: 0, 5: 2} if partly else {0: 0},
        )
        partly = (secondary,)
        primary.append(first)
        across.append(sides)
    arrived = exchange(primary, secondary, across)
    sums = first_sums(sums_of(sectioned))
    partial = call(
        local_kernel, "local", whole, cells_shape, sectioned, sums, cells,
        scratch=table_scratch, static=(vel_size, levels, True),
    )
    result = ()
    for c, (begin, end) in enumerate(bounds):
        result = (
            call(
                finish_kernel, "finish", outside, shape(*table.shape),
                partial, sectioned, *arrived[c], *result,
                scratch=[
                    held(end - begin),
                    pltpu.VMEM((TILES, ROWS * ROWS, LANES), f32),
                    copies(end - begin),
                ],
                static=(vel_size, levels, begin, end, int(c in PARTED)),
                aliases={2 + len(arrived[c]): 0} if result else {},
            ),
        )
    return result[0]


def solution(mesh):
    sizes = tuple(mesh.shape[name] for name in ("vel", "sx", "sy"))
    return jax.shard_map(
        functools.partial(local, sizes),
        mesh=mesh,
        in_specs=(P("sx", "sy", "vel"),),
        out_specs=P("sx", "sy", "vel"),
        check_vma=False,
    )
```

```python
import functools
import math

import jax
import jax.numpy as jnp
from jax import lax
from jax.experimental import pallas as pl
from jax.experimental.pallas import tpu as pltpu
from jax.sharding import PartitionSpec as P

KV = 32
SPLIT = (5, 8)
PARTED = ()
LANES = 128
ROWS = 8

vel_bound = 4.5
time_step = 0.25 / 4.5
collision_interval = 0.25
power_law_index = 0.81
diffusivity_ratio = 2.0 / 3.0
step = vel_bound / KV
weight = (2.0 * vel_bound / KV) ** 3 * (2.0 * math.pi) ** (-1.5)
f32 = jnp.float32

TILES = KV * KV // LANES
HALF = TILES // 2
PER_TILE = LANES // KV
SLOTS = LANES // ROWS


def limited(p, q):
    return jnp.maximum(jnp.minimum(p, jnp.maximum(q, 0.0)), jnp.minimum(q, 0.0))


def lane_index():
    return lax.broadcasted_iota(jnp.int32, (ROWS, LANES), 1)


def component(digit):
    return (2 * digit + 1 - KV).astype(f32) * step


def lane_components(tile):
    lane = lane_index()
    return component(tile * PER_TILE + lane // KV), component(lane % KV)


def flow_of(vel_size):
    return lax.axis_index("vel") >= vel_size // 2


def order_of(flow):
    return [jnp.where(flow, k, ROWS - 1 - k) for k in range(ROWS)]


def row_of(x):
    return pl.ds(pl.multiple_of(x * ROWS, ROWS), ROWS)


def column_of(y):
    return pl.ds(y, ROWS, stride=ROWS)


def lanes_of(tile):
    return pl.ds(pl.multiple_of(tile * LANES, LANES), LANES)


def columns_in_order(sign):
    return range(ROWS) if sign else range(ROWS - 1, -1, -1)


def inner_changes(cells):
    slopes = [cells[k + 1] - cells[k] for k in range(ROWS - 1)]
    faces = [cells[k] + 0.5 * limited(slopes[k - 1], slopes[k]) for k in range(1, ROWS - 1)]
    middle = [faces[k] - faces[k - 1] for k in range(1, ROWS - 2)]
    return [faces[0], *middle, -faces[-1]]


def outer_changes(far, near, p0, p1, p6, p7, ahead):
    slope = p0 - near
    entry = near + 0.5 * limited(near - far, slope)
    first = p0 + 0.5 * limited(slope, p1 - p0)
    leave = p7 + 0.5 * limited(p7 - p6, ahead - p7)
    return first - entry, -first, leave


def send_y(source, pair, low, high, across):
    across[0][pair, 0] = source[high, column_of(6), :]
    across[0][pair, 1] = source[high, column_of(7), :]
    across[0][pair, 2] = source[low, column_of(7), :]
    across[1][pair, 0] = source[low, column_of(1), :]
    across[1][pair, 1] = source[low, column_of(0), :]
    across[1][pair, 2] = source[high, column_of(0), :]


def pack_kernel(vel_size, levels, bounds, table, cells, *refs):
    chunks = len(bounds)
    across, primary, secondary = refs[:chunks], refs[chunks : 2 * chunks], refs[2 * chunks]
    held, sems = refs[-2], refs[-1]
    rows = [row_of(x) for x in order_of(flow_of(vel_size))]
    width = TILES * LANES

    def copy(level):
        lanes = pl.ds(pl.multiple_of(level * width, width), width)
        return pltpu.make_async_copy(table.at[:, :, lanes], held.at[level], sems.at[level])

    for level in range(levels):
        copy(level).start()
    for c, (begin, end) in enumerate(bounds):

        def one(level, carry, c=c, begin=begin):
            copy(level).wait()
            for quarter in range(HALF):
                low = level * TILES + quarter
                high = low + HALF
                for tile, sub in ((low, quarter), (high, quarter + HALF)):
                    for x in range(ROWS):
                        cells[tile, x * ROWS : (x + 1) * ROWS, :] = held[
                            level, x, :, sub * LANES : (sub + 1) * LANES
                        ]
                    primary[c][tile - begin * TILES, 0] = cells[tile, rows[6], :]
                    primary[c][tile - begin * TILES, 1] = cells[tile, rows[7], :]
                    secondary[tile] = cells[tile, rows[0], :]
                send_y(cells, (level - begin) * HALF + quarter, low, high, halves(across[c : c + 1]))
            return carry

        lax.fori_loop(begin, end, one, 0)


def halves(refs):
    return refs if len(refs) == 2 else [refs[0].at[0], refs[0].at[1]]


def sums_kernel(levels, cells, *refs):
    sums = refs[-1]
    lane = lane_index()
    base = lax.axis_index("vel") * levels
    speed = [component(base + level) for level in range(levels)]

    def one(x, total):
        acc = [jnp.zeros((ROWS, LANES), f32) for _ in range(13)]
        row = row_of(x)
        for tile in range(TILES):
            cb, ce = lane_components(tile)
            m0 = m1 = m2 = m3 = None
            for level in range(levels):
                g = cells[level * TILES + tile, row, :]
                g1 = g * speed[level]
                g2 = g1 * speed[level]
                g3 = g2 * speed[level]
                if level == 0:
                    m0, m1, m2, m3 = g, g1, g2, g3
                else:
                    m0, m1, m2, m3 = m0 + g, m1 + g1, m2 + g2, m3 + g3
            square = cb * cb + ce * ce
            b0 = cb * m0
            e0 = ce * m0
            terms = (
                m0, m1, b0, e0, m2, cb * b0, ce * e0, cb * m1, ce * m1, cb * e0,
                m3 + square * m1, cb * m2 + square * b0, ce * m2 + square * e0,
            )
            acc = [a + t for a, t in zip(acc, terms)]
        for m in range(13):
            total = jnp.where(lane == x * SLOTS + m, jnp.sum(acc[m], axis=1, keepdims=True), total)
        return total

    sums[...] = lax.fori_loop(0, ROWS, one, jnp.zeros((ROWS, LANES), f32))


def tables(parts, levels, base, scale, tab_b, tab_a, keep):
    sums = None
    for part in parts:
        for i in range(part.shape[0] // ROWS):
            more = part[i * ROWS : (i + 1) * ROWS, :]
            sums = more if sums is None else sums + more
    sums = sums * weight
    for x in range(ROWS):
        m = [
            jnp.broadcast_to(sums[:, x * SLOTS + i : x * SLOTS + i + 1], (ROWS, LANES))
            for i in range(13)
        ]
        n = m[0]
        inverse = 1.0 / n
        u = [m[i] * inverse for i in (1, 2, 3)]
        uu = u[0] * u[0] + u[1] * u[1] + u[2] * u[2]
        energy = m[4] + m[5] + m[6]
        temp = (energy * inverse - uu) * (1.0 / 3.0)
        rows = ((4, 7, 8), (7, 5, 9), (8, 9, 6))
        q = []
        for i in range(3):
            r = rows[i]
            stress = m[r[0]] * u[0] + m[r[1]] * u[1] + m[r[2]] * u[2]
            q.append(0.5 * (m[10 + i] - 2.0 * stress - u[i] * energy + 2.0 * n * u[i] * uu))
        log_temp = jnp.log(temp)
        rate = n * jnp.exp((1.0 - power_law_index) * log_temp) * (time_step / collision_interval)
        cold = 1.0 / temp
        half_cold = 0.5 * cold
        size = scale * rate * n * (cold * lax.rsqrt(temp))
        lift = (1.0 - diffusivity_ratio) / (5.0 * n * temp * temp)
        keep[x] = scale * (1.0 - rate)
        ql = [part * lift for part in q]
        for tile in range(TILES):
            cb, ce = lane_components(tile)
            db, de = cb - u[1], ce - u[2]
            square = db * db + de * de
            tab_b[x, tile, 0] = size * jnp.exp(-square * half_cold)
            tab_b[x, tile, 1] = db * ql[1] + de * ql[2]
            tab_b[x, tile, 2] = square * cold - 5.0
        for level in range(levels):
            da = component(base + level) - u[0]
            square = da * da
            tab_a[x, level, 0] = jnp.exp(-square * half_cold)
            tab_a[x, level, 1] = da * ql[0]
            tab_a[x, level, 2] = square * cold


def speeds(base, level, quarter, sign, scale):
    b_digit = quarter * PER_TILE + lane_index() // KV + sign * (KV // 2)
    a_speed = jnp.abs(component(base + level)) * (time_step * scale)
    return a_speed, jnp.abs(component(b_digit)) * (time_step * scale)


def local_kernel(vel_size, levels, last, *refs):
    cells, parts, first, (out, tab_b, tab_a, keep, side) = refs[0], refs[1:2], refs[2:-5], refs[-5:]
    scale = 0.5 if last else 1.0
    base = lax.axis_index("vel") * levels
    tables(parts, levels, base, scale, tab_b, tab_a, keep)
    xs = order_of(flow_of(vel_size))
    rows = [row_of(x) for x in xs]
    for sign in (0, 1):
        side[sign] = jnp.zeros((ROWS * ROWS, LANES), f32)

    def one(i, carry):
        level, quarter = i // HALF, i % HALF
        for sign in (0, 1):
            sub = quarter + sign * HALF
            tile = level * TILES + sub
            a_speed, b_speed = speeds(base, level, quarter, sign, scale)
            ys = columns_in_order(sign)
            line = [cells[tile, column_of(y), :] for y in ys]
            for k, change in enumerate(inner_changes(line)):
                side[sign, column_of(ys[k + 1]), :] = b_speed * change
            line = [cells[tile, row, :] for row in rows]
            changes = inner_changes(line)
            for k in range(ROWS):
                x, row = xs[k], rows[k]
                source = tab_a[x, level, 0] * tab_b[x, sub, 0]
                bend = tab_a[x, level, 1] + tab_b[x, sub, 1]
                wide = tab_a[x, level, 2] + tab_b[x, sub, 2]
                new = line[k] * keep[x] + (source + source * (bend * wide))
                moved = side[sign, row, :]
                if k > 0:
                    moved = moved + a_speed * changes[k - 1]
                new = new - moved
                if last:
                    new = 0.5 * first[0][tile, row, :] + new
                out[tile, row, :] = new
        return carry

    lax.fori_loop(0, levels * HALF, one, 0)


def edge_changes(cells, tile, i, sign, rows, speed, from_x, from_y):
    a_speed, b_speed = speed
    mine, other = 1 - sign, sign
    ys = columns_in_order(sign)
    line = [cells[tile, column_of(ys[k]), :] for k in (0, 1, 6, 7)]
    across = outer_changes(from_y[mine][i, 0], from_y[mine][i, 1], *line, from_y[other][i, 2])
    line = [cells[tile, rows[k], :] for k in (0, 1, 6, 7)]
    far, near, ahead = from_x(tile)
    along = outer_changes(far, near, *line, ahead)
    return [a_speed * c for c in along], [b_speed * c for c in across]


EDGE = (0, 1, ROWS - 1)
GROUP = 1


def correct_kernel(vel_size, levels, start, stop, parted, partial, cells, from_x1, from_x2, from_y, *refs):
    across = halves(refs[-1 - parted :])
    out, primary, secondary = refs[-4 - parted : -1 - parted]
    from_y = halves([from_y])
    base = lax.axis_index("vel") * levels
    xs = order_of(flow_of(vel_size))
    rows = [row_of(x) for x in xs]

    def from_x(tile):
        here = tile - start * TILES
        return from_x1[here, 0], from_x1[here, 1], from_x2[tile]

    def one(level, carry):
        for group in range(0, HALF, GROUP):
            changes = []
            for quarter in range(group, group + GROUP):
                for sign in (0, 1):
                    tile = level * TILES + quarter + sign * HALF
                    along, sides = edge_changes(
                        cells, tile, (level - start) * HALF + quarter, sign, rows,
                        speeds(base, level, quarter, sign, 1.0), from_x, from_y,
                    )
                    changes.append((tile, columns_in_order(sign), along, sides))
            old = [[out[t, column_of(ys[k]), :] for k in EDGE] for t, ys, _, _ in changes]
            for (t, ys, _, sides), before in zip(changes, old):
                for k, value, change in zip(EDGE, before, sides):
                    out[t, column_of(ys[k]), :] = value - change
            old = [[out[t, rows[k], :] for k in EDGE] for t, _, _, _ in changes]
            for (t, _, along, _), before in zip(changes, old):
                mine = t - start * TILES
                new = [value - change for value, change in zip(before, along)]
                for k, value in zip(EDGE, new):
                    out[t, rows[k], :] = value
                secondary[t] = new[0]
                primary[mine, 1] = new[2]
            for t, _, _, _ in changes:
                primary[t - start * TILES, 0] = out[t, rows[6], :]
            for quarter in range(group, group + GROUP):
                low = level * TILES + quarter
                send_y(out, (level - start) * HALF + quarter, low, low + HALF, across)
        return carry

    lax.fori_loop(start, stop, one, 0)


def finish_kernel(vel_size, levels, start, stop, parted, partial, cells, from_x1, from_x2, *refs):
    from_y = halves(refs[: 1 + parted])
    result, held, side, sems = refs[-4:]
    base = lax.axis_index("vel") * levels
    xs = order_of(flow_of(vel_size))
    rows = [row_of(x) for x in xs]
    width = TILES * LANES
    for sub in range(TILES):
        side[sub] = jnp.zeros((ROWS * ROWS, LANES), f32)

    def from_x(tile):
        here = tile - start * TILES
        return from_x1[here, 0], from_x1[here, 1], from_x2[tile]

    def copy(level):
        lanes = pl.ds(pl.multiple_of(level * width, width), width)
        here = level - start
        return pltpu.make_async_copy(held.at[here], result.at[:, :, lanes], sems.at[here])

    def one(level, carry):
        for quarter in range(HALF):
            for sign in (0, 1):
                sub = quarter + sign * HALF
                tile = level * TILES + sub
                ys = columns_in_order(sign)
                along, across = edge_changes(
                    cells, tile, (level - start) * HALF + quarter, sign, rows,
                    speeds(base, level, quarter, sign, 0.5), from_x, from_y,
                )
                for k, change in zip(EDGE, across):
                    side[sub, column_of(ys[k]), :] = change
                extra = dict(zip(EDGE, along))
                for k in range(ROWS):
                    new = partial[tile, rows[k], :] - side[sub, rows[k], :]
                    if k in extra:
                        new = new - extra[k]
                    held[level - start, xs[k], :, sub * LANES : (sub + 1) * LANES] = new
        copy(level).start()
        return carry

    lax.fori_loop(start, stop, one, 0)
    for level in range(start, stop):
        copy(level).wait()


def local(sizes, table):
    vel_size, sx_size, sy_size = sizes
    cells_x, cells_y, count = table.shape
    levels = count // (KV * KV)
    assert cells_x == ROWS and cells_y == ROWS and vel_size % 2 == 0
    assert count == levels * KV * KV
    first_part = levels * SPLIT[0] // SPLIT[1]
    bounds = [(0, first_part), (first_part, levels)] if 0 < first_part < levels else [(0, levels)]
    chunks = len(bounds)
    tiles = levels * TILES
    shape = lambda *dims: jax.ShapeDtypeStruct(dims, f32)
    cells_shape = shape(tiles, ROWS * ROWS, LANES)
    across_shape = [shape(2, (b - a) * HALF, 3, ROWS, LANES) for a, b in bounds]
    primary_shape = [shape((b - a) * TILES, 2, ROWS, LANES) for a, b in bounds]
    secondary_shape = shape(tiles, ROWS, LANES)
    whole = pl.BlockSpec(memory_space=pltpu.VMEM)
    outside = pl.BlockSpec(memory_space=pltpu.HBM)
    half = vel_size // 2

    def call(kernel, name, ins, outs, *args, scratch=(), aliases={}, static=()):
        specs = [outside if a.shape == table.shape else whole for a in args]
        return pl.pallas_call(
            functools.partial(kernel, *static),
            out_shape=outs,
            in_specs=specs,
            out_specs=ins,
            scratch_shapes=list(scratch),
            input_output_aliases=aliases,
            compiler_params=pltpu.CompilerParams(vmem_limit_bytes=16 * 1024 * 1024),
            name=name,
        )(*args)

    def along_x(array, sign):
        pairs = []
        for v in range(vel_size):
            way = sign if v >= half else -sign
            pairs += [(v * sx_size + i, v * sx_size + (i + way) % sx_size) for i in range(sx_size)]
        return lax.ppermute(array, ("vel", "sx"), pairs)

    def along_y(arrays):
        ways = [[(i, (i + way) % sy_size) for i in range(sy_size)] for way in (1, -1)]
        if len(arrays) == 2:
            return tuple(lax.ppermute(a, "sy", way) for a, way in zip(arrays, ways))
        if sy_size == 2:
            return (lax.ppermute(arrays[0], "sy", ways[0]),)
        return (jnp.stack([lax.ppermute(arrays[0][i], "sy", ways[i]) for i in (0, 1)]),)

    def exchange(primary, secondary, across):
        behind = along_x(secondary, -1)
        return [(along_x(p, 1), behind, *along_y(a)) for p, a in zip(primary, across)]

    def sums_of(cells, *after):
        return call(sums_kernel, "sums", whole, shape(ROWS, LANES), cells, *after, static=(levels,))

    def first_sums(sums):
        if vel_size > 4:
            return lax.psum(sums, "vel")
        return lax.all_gather(sums, "vel", axis=0, tiled=True)

    def second_sums(sums):
        if vel_size & (vel_size - 1):
            return lax.psum(sums, "vel")
        d = 1
        while d < vel_size:
            sums = sums + lax.ppermute(sums, "vel", [(i, i ^ d) for i in range(vel_size)])
            d *= 2
        return sums

    table_scratch = [
        pltpu.VMEM((ROWS, TILES, 3, ROWS, LANES), f32),
        pltpu.VMEM((ROWS, levels, 3, ROWS, LANES), f32),
        pltpu.VMEM((ROWS, ROWS, LANES), f32),
        pltpu.VMEM((2, ROWS * ROWS, LANES), f32),
    ]
    held = lambda count: pltpu.VMEM((count, ROWS, ROWS, TILES * LANES), f32)
    copies = lambda count: pltpu.SemaphoreType.DMA((count,))

    cells, *messages, secondary = call(
        pack_kernel, "pack", [whole] * (2 * chunks + 2),
        [cells_shape] + across_shape + primary_shape + [secondary_shape],
        pltpu.with_memory_space_constraint(table, pltpu.HBM), scratch=[held(levels), copies(levels)], static=(vel_size, levels, bounds),
    )
    arrived = exchange(messages[chunks:], secondary, [(m,) for m in messages[:chunks]])
    sectioned = call(
        local_kernel, "local", whole, cells_shape, cells, first_sums(sums_of(cells)),
        scratch=table_scratch, static=(vel_size, levels, False),
    )
    primary, across, partly = [], [], ()
    for c, (begin, end) in enumerate(bounds):
        parted = int(c in PARTED)
        one_way = shape((end - begin) * HALF, 3, ROWS, LANES)
        sectioned, first, secondary, *sides = call(
            correct_kernel, "correct", [whole] * (4 + parted),
            [cells_shape, primary_shape[c], secondary_shape]
            + ([one_way] * 2 if parted else [across_shape[c]]),
            sectioned, cells, *arrived[c], *partly,
            static=(vel_size, levels, begin, end, parted),
            aliases={0: 0, 5: 2} if partly else {0: 0},
        )
        partly = (secondary,)
        primary.append(first)
        across.append(sides)
    arrived = exchange(primary, secondary, across)
    sums = first_sums(sums_of(sectioned))
    partial = call(
        local_kernel, "local", whole, cells_shape, sectioned, sums, cells,
        scratch=table_scratch, static=(vel_size, levels, True),
    )
    result = ()
    for c, (begin, end) in enumerate(bounds):
        result = (
            call(
                finish_kernel, "finish", outside, shape(*table.shape),
                partial, sectioned, *arrived[c], *result,
                scratch=[
                    held(end - begin),
                    pltpu.VMEM((TILES, ROWS * ROWS, LANES), f32),
                    copies(end - begin),
                ],
                static=(vel_size, levels, begin, end, int(c in PARTED)),
                aliases={2 + len(arrived[c]): 0} if result else {},
            ),
        )
    return result[0]


def solution(mesh):
    sizes = tuple(mesh.shape[name] for name in ("vel", "sx", "sy"))
    return jax.shard_map(
        functools.partial(local, sizes),
        mesh=mesh,
        in_specs=(P("sx", "sy", "vel"),),
        out_specs=P("sx", "sy", "vel"),
        check_vma=False,
    )
```

```python
import functools
import math

import jax
import jax.numpy as jnp
from jax import lax
from jax.experimental import pallas as pl
from jax.experimental.pallas import tpu as pltpu
from jax.sharding import PartitionSpec as P

KV = 32
SPLIT = (5, 8)
LANES = 128
ROWS = 8

vel_bound = 4.5
time_step = 0.25 / 4.5
collision_interval = 0.25
power_law_index = 0.81
diffusivity_ratio = 2.0 / 3.0
step = vel_bound / KV
weight = (2.0 * vel_bound / KV) ** 3 * (2.0 * math.pi) ** (-1.5)
f32 = jnp.float32

TILES = KV * KV // LANES
HALF = TILES // 2
PER_TILE = LANES // KV
SLOTS = LANES // ROWS


def limited(p, q):
    return jnp.maximum(jnp.minimum(p, jnp.maximum(q, 0.0)), jnp.minimum(q, 0.0))


def lane_index():
    return lax.broadcasted_iota(jnp.int32, (ROWS, LANES), 1)


def component(digit):
    return (2 * digit + 1 - KV).astype(f32) * step


def lane_components(tile):
    lane = lane_index()
    return component(tile * PER_TILE + lane // KV), component(lane % KV)


def flow_of(vel_size):
    return lax.axis_index("vel") >= vel_size // 2


def order_of(flow):
    return [jnp.where(flow, k, ROWS - 1 - k) for k in range(ROWS)]


def row_of(x):
    return pl.ds(pl.multiple_of(x * ROWS, ROWS), ROWS)


def column_of(y):
    return pl.ds(y, ROWS, stride=ROWS)


def lanes_of(tile):
    return pl.ds(pl.multiple_of(tile * LANES, LANES), LANES)


def columns_in_order(sign):
    return range(ROWS) if sign else range(ROWS - 1, -1, -1)


def inner_changes(cells):
    slopes = [cells[k + 1] - cells[k] for k in range(ROWS - 1)]
    faces = [cells[k] + 0.5 * limited(slopes[k - 1], slopes[k]) for k in range(1, ROWS - 1)]
    middle = [faces[k] - faces[k - 1] for k in range(1, ROWS - 2)]
    return [faces[0], *middle, -faces[-1]]


def outer_changes(far, near, p0, p1, p6, p7, ahead):
    slope = p0 - near
    entry = near + 0.5 * limited(near - far, slope)
    first = p0 + 0.5 * limited(slope, p1 - p0)
    leave = p7 + 0.5 * limited(p7 - p6, ahead - p7)
    return first - entry, -first, leave


def send_y(source, pair, low, high, across):
    across[0][pair, 0] = source[high, column_of(6), :]
    across[0][pair, 1] = source[high, column_of(7), :]
    across[0][pair, 2] = source[low, column_of(7), :]
    across[1][pair, 0] = source[low, column_of(1), :]
    across[1][pair, 1] = source[low, column_of(0), :]
    across[1][pair, 2] = source[high, column_of(0), :]


def pack_kernel(vel_size, levels, bounds, table, cells, *refs):
    chunks = len(bounds)
    across, primary, secondary = refs[:chunks], refs[chunks], refs[chunks + 1]
    held, sems = refs[-2], refs[-1]
    rows = [row_of(x) for x in order_of(flow_of(vel_size))]
    width = TILES * LANES

    def copy(level):
        lanes = pl.ds(pl.multiple_of(level * width, width), width)
        return pltpu.make_async_copy(table.at[:, :, lanes], held.at[level], sems.at[level])

    for level in range(levels):
        copy(level).start()
    for c, (begin, end) in enumerate(bounds):

        def one(level, carry, c=c, begin=begin):
            copy(level).wait()
            for quarter in range(HALF):
                low = level * TILES + quarter
                high = low + HALF
                for tile, sub in ((low, quarter), (high, quarter + HALF)):
                    for x in range(ROWS):
                        cells[tile, x * ROWS : (x + 1) * ROWS, :] = held[
                            level, x, :, sub * LANES : (sub + 1) * LANES
                        ]
                    if c == 0:
                        primary[tile, 0] = cells[tile, rows[6], :]
                        primary[tile, 1] = cells[tile, rows[7], :]
                    secondary[tile] = cells[tile, rows[0], :]
                send_y(cells, (level - begin) * HALF + quarter, low, high, halves(across[c]))
            return carry

        lax.fori_loop(begin, end, one, 0)


def late_kernel(vel_size, begin, end, cells, after, primary):
    rows = [row_of(x) for x in order_of(flow_of(vel_size))]

    def one(level, carry):
        for sub in range(TILES):
            tile = level * TILES + sub
            primary[tile - begin * TILES, 0] = cells[tile, rows[6], :]
            primary[tile - begin * TILES, 1] = cells[tile, rows[7], :]
        return carry

    lax.fori_loop(begin, end, one, 0)


def halves(across):
    return across.at[0], across.at[1]


def sums_kernel(levels, cells, sums):
    lane = lane_index()
    base = lax.axis_index("vel") * levels
    speed = [component(base + level) for level in range(levels)]

    def one(x, total):
        acc = [jnp.zeros((ROWS, LANES), f32) for _ in range(13)]
        row = row_of(x)
        for tile in range(TILES):
            cb, ce = lane_components(tile)
            m0 = m1 = m2 = m3 = None
            for level in range(levels):
                g = cells[level * TILES + tile, row, :]
                g1 = g * speed[level]
                g2 = g1 * speed[level]
                g3 = g2 * speed[level]
                if level == 0:
                    m0, m1, m2, m3 = g, g1, g2, g3
                else:
                    m0, m1, m2, m3 = m0 + g, m1 + g1, m2 + g2, m3 + g3
            square = cb * cb + ce * ce
            b0 = cb * m0
            e0 = ce * m0
            terms = (
                m0, m1, b0, e0, m2, cb * b0, ce * e0, cb * m1, ce * m1, cb * e0,
                m3 + square * m1, cb * m2 + square * b0, ce * m2 + square * e0,
            )
            acc = [a + t for a, t in zip(acc, terms)]
        for m in range(13):
            total = jnp.where(lane == x * SLOTS + m, jnp.sum(acc[m], axis=1, keepdims=True), total)
        return total

    sums[...] = lax.fori_loop(0, ROWS, one, jnp.zeros((ROWS, LANES), f32))


def tables(parts, levels, base, scale, tab_b, tab_a, keep):
    sums = None
    for part in parts:
        for i in range(part.shape[0] // ROWS):
            more = part[i * ROWS : (i + 1) * ROWS, :]
            sums = more if sums is None else sums + more
    sums = sums * weight
    for x in range(ROWS):
        m = [
            jnp.broadcast_to(sums[:, x * SLOTS + i : x * SLOTS + i + 1], (ROWS, LANES))
            for i in range(13)
        ]
        n = m[0]
        inverse = 1.0 / n
        u = [m[i] * inverse for i in (1, 2, 3)]
        uu = u[0] * u[0] + u[1] * u[1] + u[2] * u[2]
        energy = m[4] + m[5] + m[6]
        temp = (energy * inverse - uu) * (1.0 / 3.0)
        rows = ((4, 7, 8), (7, 5, 9), (8, 9, 6))
        q = []
        for i in range(3):
            r = rows[i]
            stress = m[r[0]] * u[0] + m[r[1]] * u[1] + m[r[2]] * u[2]
            q.append(0.5 * (m[10 + i] - 2.0 * stress - u[i] * energy + 2.0 * n * u[i] * uu))
        log_temp = jnp.log(temp)
        rate = n * jnp.exp((1.0 - power_law_index) * log_temp) * (time_step / collision_interval)
        cold = 1.0 / temp
        half_cold = 0.5 * cold
        size = scale * rate * n * (cold * lax.rsqrt(temp))
        lift = (1.0 - diffusivity_ratio) / (5.0 * n * temp * temp)
        keep[x] = scale * (1.0 - rate)
        ql = [part * lift for part in q]
        for tile in range(TILES):
            cb, ce = lane_components(tile)
            db, de = cb - u[1], ce - u[2]
            square = db * db + de * de
            tab_b[x, tile, 0] = size * jnp.exp(-square * half_cold)
            tab_b[x, tile, 1] = db * ql[1] + de * ql[2]
            tab_b[x, tile, 2] = square * cold - 5.0
        for level in range(levels):
            da = component(base + level) - u[0]
            square = da * da
            tab_a[x, level, 0] = jnp.exp(-square * half_cold)
            tab_a[x, level, 1] = da * ql[0]
            tab_a[x, level, 2] = square * cold


def speeds(base, level, quarter, sign, scale):
    b_digit = quarter * PER_TILE + lane_index() // KV + sign * (KV // 2)
    a_speed = jnp.abs(component(base + level)) * (time_step * scale)
    return a_speed, jnp.abs(component(b_digit)) * (time_step * scale)


def local_kernel(vel_size, levels, last, *refs):
    cells, parts, first, (out, tab_b, tab_a, keep, side) = refs[0], refs[1:2], refs[2:-5], refs[-5:]
    scale = 0.5 if last else 1.0
    base = lax.axis_index("vel") * levels
    tables(parts, levels, base, scale, tab_b, tab_a, keep)
    xs = order_of(flow_of(vel_size))
    rows = [row_of(x) for x in xs]
    for sign in (0, 1):
        side[sign] = jnp.zeros((ROWS * ROWS, LANES), f32)

    def one(i, carry):
        level, quarter = i // HALF, i % HALF
        for sign in (0, 1):
            sub = quarter + sign * HALF
            tile = level * TILES + sub
            a_speed, b_speed = speeds(base, level, quarter, sign, scale)
            ys = columns_in_order(sign)
            line = [cells[tile, column_of(y), :] for y in ys]
            for k, change in enumerate(inner_changes(line)):
                side[sign, column_of(ys[k + 1]), :] = b_speed * change
            line = [cells[tile, row, :] for row in rows]
            changes = inner_changes(line)
            for k in range(ROWS):
                x, row = xs[k], rows[k]
                source = tab_a[x, level, 0] * tab_b[x, sub, 0]
                bend = tab_a[x, level, 1] + tab_b[x, sub, 1]
                wide = tab_a[x, level, 2] + tab_b[x, sub, 2]
                new = line[k] * keep[x] + (source + source * (bend * wide))
                moved = side[sign, row, :]
                if k > 0:
                    moved = moved + a_speed * changes[k - 1]
                new = new - moved
                if last:
                    new = 0.5 * first[0][tile, row, :] + new
                out[tile, row, :] = new
        return carry

    lax.fori_loop(0, levels * HALF, one, 0)


def edge_changes(cells, tile, i, sign, rows, speed, from_x, from_y):
    a_speed, b_speed = speed
    mine, other = 1 - sign, sign
    ys = columns_in_order(sign)
    line = [cells[tile, column_of(ys[k]), :] for k in (0, 1, 6, 7)]
    across = outer_changes(from_y[mine][i, 0], from_y[mine][i, 1], *line, from_y[other][i, 2])
    line = [cells[tile, rows[k], :] for k in (0, 1, 6, 7)]
    far, near, ahead = from_x(tile)
    along = outer_changes(far, near, *line, ahead)
    return [a_speed * c for c in along], [b_speed * c for c in across]


EDGE = (0, 1, ROWS - 1)
GROUP = 1


def correct_kernel(vel_size, levels, start, stop, partial, cells, from_x1, from_x2, from_y, *refs):
    out, primary, secondary, across = refs[-4:]
    across, from_y = halves(across), halves(from_y)
    base = lax.axis_index("vel") * levels
    xs = order_of(flow_of(vel_size))
    rows = [row_of(x) for x in xs]

    def from_x(tile):
        here = tile - start * TILES
        return from_x1[here, 0], from_x1[here, 1], from_x2[tile]

    def one(level, carry):
        for group in range(0, HALF, GROUP):
            changes = []
            for quarter in range(group, group + GROUP):
                for sign in (0, 1):
                    tile = level * TILES + quarter + sign * HALF
                    along, sides = edge_changes(
                        cells, tile, (level - start) * HALF + quarter, sign, rows,
                        speeds(base, level, quarter, sign, 1.0), from_x, from_y,
                    )
                    changes.append((tile, columns_in_order(sign), along, sides))
            old = [[out[t, column_of(ys[k]), :] for k in EDGE] for t, ys, _, _ in changes]
            for (t, ys, _, sides), before in zip(changes, old):
                for k, value, change in zip(EDGE, before, sides):
                    out[t, column_of(ys[k]), :] = value - change
            old = [[out[t, rows[k], :] for k in EDGE] for t, _, _, _ in changes]
            for (t, _, along, _), before in zip(changes, old):
                mine = t - start * TILES
                new = [value - change for value, change in zip(before, along)]
                for k, value in zip(EDGE, new):
                    out[t, rows[k], :] = value
                secondary[t] = new[0]
                primary[mine, 1] = new[2]
            for t, _, _, _ in changes:
                primary[t - start * TILES, 0] = out[t, rows[6], :]
            for quarter in range(group, group + GROUP):
                low = level * TILES + quarter
                send_y(out, (level - start) * HALF + quarter, low, low + HALF, across)
        return carry

    lax.fori_loop(start, stop, one, 0)


def finish_kernel(vel_size, levels, start, stop, partial, cells, from_x1, from_x2, from_y, *refs):
    from_y = halves(from_y)
    result, held, side, sems = refs[-4:]
    base = lax.axis_index("vel") * levels
    xs = order_of(flow_of(vel_size))
    rows = [row_of(x) for x in xs]
    width = TILES * LANES
    for sub in range(TILES):
        side[sub] = jnp.zeros((ROWS * ROWS, LANES), f32)

    def from_x(tile):
        here = tile - start * TILES
        return from_x1[here, 0], from_x1[here, 1], from_x2[tile]

    def copy(level):
        lanes = pl.ds(pl.multiple_of(level * width, width), width)
        here = level - start
        return pltpu.make_async_copy(held.at[here], result.at[:, :, lanes], sems.at[here])

    def one(level, carry):
        for quarter in range(HALF):
            for sign in (0, 1):
                sub = quarter + sign * HALF
                tile = level * TILES + sub
                ys = columns_in_order(sign)
                along, across = edge_changes(
                    cells, tile, (level - start) * HALF + quarter, sign, rows,
                    speeds(base, level, quarter, sign, 0.5), from_x, from_y,
                )
                for k, change in zip(EDGE, across):
                    side[sub, column_of(ys[k]), :] = change
                extra = dict(zip(EDGE, along))
                for k in range(ROWS):
                    new = partial[tile, rows[k], :] - side[sub, rows[k], :]
                    if k in extra:
                        new = new - extra[k]
                    held[level - start, xs[k], :, sub * LANES : (sub + 1) * LANES] = new
        copy(level).start()
        return carry

    lax.fori_loop(start, stop, one, 0)
    for level in range(start, stop):
        copy(level).wait()


def local(sizes, table):
    vel_size, sx_size, sy_size = sizes
    cells_x, cells_y, count = table.shape
    levels = count // (KV * KV)
    assert cells_x == ROWS and cells_y == ROWS and vel_size % 2 == 0
    assert count == levels * KV * KV
    first_part = levels * SPLIT[0] // SPLIT[1]
    bounds = [(0, first_part), (first_part, levels)] if 0 < first_part < levels else [(0, levels)]
    chunks = len(bounds)
    tiles = levels * TILES
    shape = lambda *dims: jax.ShapeDtypeStruct(dims, f32)
    cells_shape = shape(tiles, ROWS * ROWS, LANES)
    across_shape = [shape(2, (b - a) * HALF, 3, ROWS, LANES) for a, b in bounds]
    primary_shape = [shape((b - a) * TILES, 2, ROWS, LANES) for a, b in bounds]
    secondary_shape = shape(tiles, ROWS, LANES)
    whole = pl.BlockSpec(memory_space=pltpu.VMEM)
    outside = pl.BlockSpec(memory_space=pltpu.HBM)
    half = vel_size // 2

    def call(kernel, name, ins, outs, *args, scratch=(), aliases={}, static=()):
        specs = [outside if a.shape == table.shape else whole for a in args]
        return pl.pallas_call(
            functools.partial(kernel, *static),
            out_shape=outs,
            in_specs=specs,
            out_specs=ins,
            scratch_shapes=list(scratch),
            input_output_aliases=aliases,
            compiler_params=pltpu.CompilerParams(vmem_limit_bytes=16 * 1024 * 1024),
            name=name,
        )(*args)

    def along_x(array, sign):
        pairs = []
        for v in range(vel_size):
            way = sign if v >= half else -sign
            pairs += [(v * sx_size + i, v * sx_size + (i + way) % sx_size) for i in range(sx_size)]
        return lax.ppermute(array, ("vel", "sx"), pairs)

    def along_y(array):
        ways = [[(i, (i + way) % sy_size) for i in range(sy_size)] for way in (1, -1)]
        if sy_size == 2:
            return lax.ppermute(array, "sy", ways[0])
        return jnp.stack([lax.ppermute(array[i], "sy", ways[i]) for i in (0, 1)])

    def exchange(primary, secondary, across):
        behind = along_x(secondary, -1)
        return [(along_x(p, 1), behind, along_y(a)) for p, a in zip(primary, across)]

    def sums_of(cells):
        return call(sums_kernel, "sums", whole, shape(ROWS, LANES), cells, static=(levels,))

    def first_sums(sums):
        if vel_size > 4:
            return lax.psum(sums, "vel")
        return lax.all_gather(sums, "vel", axis=0, tiled=True)

    table_scratch = [
        pltpu.VMEM((ROWS, TILES, 3, ROWS, LANES), f32),
        pltpu.VMEM((ROWS, levels, 3, ROWS, LANES), f32),
        pltpu.VMEM((ROWS, ROWS, LANES), f32),
        pltpu.VMEM((2, ROWS * ROWS, LANES), f32),
    ]
    held = lambda count: pltpu.VMEM((count, ROWS, ROWS, TILES * LANES), f32)
    copies = lambda count: pltpu.SemaphoreType.DMA((count,))

    cells, *across, primary, secondary = call(
        pack_kernel, "pack", [whole] * (chunks + 3),
        [cells_shape] + across_shape + [primary_shape[0], secondary_shape],
        pltpu.with_memory_space_constraint(table, pltpu.HBM),
        scratch=[held(levels), copies(levels)], static=(vel_size, levels, bounds),
    )
    sums = first_sums(sums_of(cells))
    primary = [primary]
    for c in range(1, chunks):
        primary.append(
            call(
                late_kernel, "late", whole, primary_shape[c], cells, sums,
                static=(vel_size, *bounds[c]),
            )
        )
    arrived = exchange(primary, secondary, across)
    sectioned = call(
        local_kernel, "local", whole, cells_shape, cells, sums,
        scratch=table_scratch, static=(vel_size, levels, False),
    )
    primary, across, partly = [], [], ()
    for c, (begin, end) in enumerate(bounds):
        sectioned, first, secondary, last = call(
            correct_kernel, "correct", [whole] * 4,
            [cells_shape, primary_shape[c], secondary_shape, across_shape[c]],
            sectioned, cells, *arrived[c], *partly,
            static=(vel_size, levels, begin, end),
            aliases={0: 0, 5: 2} if partly else {0: 0},
        )
        partly = (secondary,)
        primary.append(first)
        across.append(last)
    arrived = exchange(primary, secondary, across)
    sums = first_sums(sums_of(sectioned))
    partial = call(
        local_kernel, "local", whole, cells_shape, sectioned, sums, cells,
        scratch=table_scratch, static=(vel_size, levels, True),
    )
    result = ()
    for c, (begin, end) in enumerate(bounds):
        result = (
            call(
                finish_kernel, "finish", outside, shape(*table.shape),
                partial, sectioned, *arrived[c], *result,
                scratch=[
                    held(end - begin),
                    pltpu.VMEM((TILES, ROWS * ROWS, LANES), f32),
                    copies(end - begin),
                ],
                static=(vel_size, levels, begin, end),
                aliases={5: 0} if result else {},
            ),
        )
    return result[0]


def solution(mesh):
    sizes = tuple(mesh.shape[name] for name in ("vel", "sx", "sy"))
    return jax.shard_map(
        functools.partial(local, sizes),
        mesh=mesh,
        in_specs=(P("sx", "sy", "vel"),),
        out_specs=P("sx", "sy", "vel"),
        check_vma=False,
    )
```

```python
import functools
import math

import jax
import jax.numpy as jnp
from jax import lax
from jax.experimental import pallas as pl
from jax.experimental.pallas import tpu as pltpu
from jax.sharding import PartitionSpec as P

KV = 32
SPLIT = (5, 8)
LANES = 128
ROWS = 8

vel_bound = 4.5
time_step = 0.25 / 4.5
collision_interval = 0.25
power_law_index = 0.81
diffusivity_ratio = 2.0 / 3.0
step = vel_bound / KV
weight = (2.0 * vel_bound / KV) ** 3 * (2.0 * math.pi) ** (-1.5)
f32 = jnp.float32

TILES = KV * KV // LANES
HALF = TILES // 2
PER_TILE = LANES // KV
SLOTS = LANES // ROWS


def limited(p, q):
    return jnp.maximum(jnp.minimum(p, jnp.maximum(q, 0.0)), jnp.minimum(q, 0.0))


def lane_index():
    return lax.broadcasted_iota(jnp.int32, (ROWS, LANES), 1)


def component(digit):
    return (2 * digit + 1 - KV).astype(f32) * step


def lane_components(tile):
    lane = lane_index()
    return component(tile * PER_TILE + lane // KV), component(lane % KV)


def flow_of(vel_size):
    return lax.axis_index("vel") >= vel_size // 2


def order_of(flow):
    return [jnp.where(flow, k, ROWS - 1 - k) for k in range(ROWS)]


def row_of(x):
    return pl.ds(pl.multiple_of(x * ROWS, ROWS), ROWS)


def column_of(y):
    return pl.ds(y, ROWS, stride=ROWS)


def lanes_of(tile):
    return pl.ds(pl.multiple_of(tile * LANES, LANES), LANES)


def columns_in_order(sign):
    return range(ROWS) if sign else range(ROWS - 1, -1, -1)


def inner_changes(cells):
    slopes = [cells[k + 1] - cells[k] for k in range(ROWS - 1)]
    faces = [cells[k] + 0.5 * limited(slopes[k - 1], slopes[k]) for k in range(1, ROWS - 1)]
    middle = [faces[k] - faces[k - 1] for k in range(1, ROWS - 2)]
    return [faces[0], *middle, -faces[-1]]


def outer_changes(far, near, p0, p1, p6, p7, ahead):
    slope = p0 - near
    entry = near + 0.5 * limited(near - far, slope)
    first = p0 + 0.5 * limited(slope, p1 - p0)
    leave = p7 + 0.5 * limited(p7 - p6, ahead - p7)
    return first - entry, -first, leave


def send_y(source, pair, low, high, across):
    across[0][pair, 0] = source[high, column_of(6), :]
    across[0][pair, 1] = source[high, column_of(7), :]
    across[0][pair, 2] = source[low, column_of(7), :]
    across[1][pair, 0] = source[low, column_of(1), :]
    across[1][pair, 1] = source[low, column_of(0), :]
    across[1][pair, 2] = source[high, column_of(0), :]


def pack_kernel(vel_size, levels, bounds, table, cells, *refs):
    chunks = len(bounds)
    across, primary, secondary = refs[:chunks], refs[chunks], refs[chunks + 1]
    held, sems = refs[-2], refs[-1]
    rows = [row_of(x) for x in order_of(flow_of(vel_size))]
    width = TILES * LANES

    def copy(level):
        lanes = pl.ds(pl.multiple_of(level * width, width), width)
        return pltpu.make_async_copy(table.at[:, :, lanes], held.at[level], sems.at[level])

    for level in range(levels):
        copy(level).start()
    for c, (begin, end) in enumerate(bounds):

        def one(level, carry, c=c, begin=begin):
            copy(level).wait()
            for quarter in range(HALF):
                low = level * TILES + quarter
                high = low + HALF
                for tile, sub in ((low, quarter), (high, quarter + HALF)):
                    for x in range(ROWS):
                        cells[tile, x * ROWS : (x + 1) * ROWS, :] = held[
                            level, x, :, sub * LANES : (sub + 1) * LANES
                        ]
                    if c == 0:
                        primary[tile, 0] = cells[tile, rows[6], :]
                        primary[tile, 1] = cells[tile, rows[7], :]
                    secondary[tile] = cells[tile, rows[0], :]
                send_y(cells, (level - begin) * HALF + quarter, low, high, halves(across[c]))
            return carry

        lax.fori_loop(begin, end, one, 0)


def late_kernel(vel_size, begin, end, cells, after, primary):
    rows = [row_of(x) for x in order_of(flow_of(vel_size))]

    def one(level, carry):
        for sub in range(TILES):
            tile = level * TILES + sub
            primary[tile - begin * TILES, 0] = cells[tile, rows[6], :]
            primary[tile - begin * TILES, 1] = cells[tile, rows[7], :]
        return carry

    lax.fori_loop(begin, end, one, 0)


def halves(across):
    return across.at[0], across.at[1]


def sums_kernel(levels, cells, sums):
    lane = lane_index()
    base = lax.axis_index("vel") * levels
    speed = [component(base + level) for level in range(levels)]

    def one(x, total):
        acc = [jnp.zeros((ROWS, LANES), f32) for _ in range(13)]
        row = row_of(x)
        for tile in range(TILES):
            cb, ce = lane_components(tile)
            m0 = m1 = m2 = m3 = None
            for level in range(levels):
                g = cells[level * TILES + tile, row, :]
                g1 = g * speed[level]
                g2 = g1 * speed[level]
                g3 = g2 * speed[level]
                if level == 0:
                    m0, m1, m2, m3 = g, g1, g2, g3
                else:
                    m0, m1, m2, m3 = m0 + g, m1 + g1, m2 + g2, m3 + g3
            square = cb * cb + ce * ce
            b0 = cb * m0
            e0 = ce * m0
            terms = (
                m0, m1, b0, e0, m2, cb * b0, ce * e0, cb * m1, ce * m1, cb * e0,
                m3 + square * m1, cb * m2 + square * b0, ce * m2 + square * e0,
            )
            acc = [a + t for a, t in zip(acc, terms)]
        for m in range(13):
            total = jnp.where(lane == x * SLOTS + m, jnp.sum(acc[m], axis=1, keepdims=True), total)
        return total

    sums[...] = lax.fori_loop(0, ROWS, one, jnp.zeros((ROWS, LANES), f32))


def tables(parts, levels, base, scale, tab_b, tab_a, keep):
    sums = None
    for part in parts:
        for i in range(part.shape[0] // ROWS):
            more = part[i * ROWS : (i + 1) * ROWS, :]
            sums = more if sums is None else sums + more
    sums = sums * weight
    for x in range(ROWS):
        m = [
            jnp.broadcast_to(sums[:, x * SLOTS + i : x * SLOTS + i + 1], (ROWS, LANES))
            for i in range(13)
        ]
        n = m[0]
        inverse = 1.0 / n
        u = [m[i] * inverse for i in (1, 2, 3)]
        uu = u[0] * u[0] + u[1] * u[1] + u[2] * u[2]
        energy = m[4] + m[5] + m[6]
        temp = (energy * inverse - uu) * (1.0 / 3.0)
        rows = ((4, 7, 8), (7, 5, 9), (8, 9, 6))
        q = []
        for i in range(3):
            r = rows[i]
            stress = m[r[0]] * u[0] + m[r[1]] * u[1] + m[r[2]] * u[2]
            q.append(0.5 * (m[10 + i] - 2.0 * stress - u[i] * energy + 2.0 * n * u[i] * uu))
        log_temp = jnp.log(temp)
        rate = n * jnp.exp((1.0 - power_law_index) * log_temp) * (time_step / collision_interval)
        cold = 1.0 / temp
        half_cold = 0.5 * cold
        size = scale * rate * n * (cold * lax.rsqrt(temp))
        lift = (1.0 - diffusivity_ratio) / (5.0 * n * temp * temp)
        keep[x] = scale * (1.0 - rate)
        ql = [part * lift for part in q]
        for tile in range(TILES):
            cb, ce = lane_components(tile)
            db, de = cb - u[1], ce - u[2]
            square = db * db + de * de
            tab_b[x, tile, 0] = size * jnp.exp(-square * half_cold)
            tab_b[x, tile, 1] = db * ql[1] + de * ql[2]
            tab_b[x, tile, 2] = square * cold - 5.0
        for level in range(levels):
            da = component(base + level) - u[0]
            square = da * da
            tab_a[x, level, 0] = jnp.exp(-square * half_cold)
            tab_a[x, level, 1] = da * ql[0]
            tab_a[x, level, 2] = square * cold


def speeds(base, level, quarter, sign, scale):
    b_digit = quarter * PER_TILE + lane_index() // KV + sign * (KV // 2)
    a_speed = jnp.abs(component(base + level)) * (time_step * scale)
    return a_speed, jnp.abs(component(b_digit)) * (time_step * scale)


def local_kernel(vel_size, levels, last, *refs):
    cells, parts, first, (out, tab_b, tab_a, keep, side) = refs[0], refs[1:2], refs[2:-5], refs[-5:]
    scale = 0.5 if last else 1.0
    base = lax.axis_index("vel") * levels
    tables(parts, levels, base, scale, tab_b, tab_a, keep)
    xs = order_of(flow_of(vel_size))
    rows = [row_of(x) for x in xs]
    for sign in (0, 1):
        side[sign] = jnp.zeros((ROWS * ROWS, LANES), f32)

    def one(i, carry):
        level, quarter = i // HALF, i % HALF
        for sign in (0, 1):
            sub = quarter + sign * HALF
            tile = level * TILES + sub
            a_speed, b_speed = speeds(base, level, quarter, sign, scale)
            ys = columns_in_order(sign)
            line = [cells[tile, column_of(y), :] for y in ys]
            for k, change in enumerate(inner_changes(line)):
                side[sign, column_of(ys[k + 1]), :] = b_speed * change
            line = [cells[tile, row, :] for row in rows]
            changes = inner_changes(line)
            for k in range(ROWS):
                x, row = xs[k], rows[k]
                source = tab_a[x, level, 0] * tab_b[x, sub, 0]
                bend = tab_a[x, level, 1] + tab_b[x, sub, 1]
                wide = tab_a[x, level, 2] + tab_b[x, sub, 2]
                new = line[k] * keep[x] + (source + source * (bend * wide))
                moved = side[sign, row, :]
                if k > 0:
                    moved = moved + a_speed * changes[k - 1]
                new = new - moved
                if last:
                    new = 0.5 * first[0][tile, row, :] + new
                out[tile, row, :] = new
        return carry

    lax.fori_loop(0, levels * HALF, one, 0)


def side_changes(cells, tile, i, sign, speed, from_y):
    mine, other = 1 - sign, sign
    ys = columns_in_order(sign)
    line = [cells[tile, column_of(ys[k]), :] for k in (0, 1, 6, 7)]
    changes = outer_changes(from_y[mine][i, 0], from_y[mine][i, 1], *line, from_y[other][i, 2])
    return [speed * change for change in changes]


def flow_changes(cells, tile, rows, speed, from_x):
    line = [cells[tile, rows[k], :] for k in (0, 1, 6, 7)]
    far, near, ahead = from_x(tile)
    return [speed * change for change in outer_changes(far, near, *line, ahead)]


def edge_changes(cells, tile, i, sign, rows, speed, from_x, from_y):
    along = flow_changes(cells, tile, rows, speed[0], from_x)
    return along, side_changes(cells, tile, i, sign, speed[1], from_y)


EDGE = (0, 1, ROWS - 1)
GROUP = 1


def correct_kernel(vel_size, levels, start, stop, partial, cells, from_x1, from_x2, from_y, *refs):
    out, primary, secondary, across = refs[-4:]
    across, from_y = halves(across), halves(from_y)
    base = lax.axis_index("vel") * levels
    xs = order_of(flow_of(vel_size))
    rows = [row_of(x) for x in xs]

    def from_x(tile):
        here = tile - start * TILES
        return from_x1[here, 0], from_x1[here, 1], from_x2[tile]

    def one(level, carry):
        for group in range(0, HALF, GROUP):
            changes = []
            for quarter in range(group, group + GROUP):
                for sign in (0, 1):
                    tile = level * TILES + quarter + sign * HALF
                    along, sides = edge_changes(
                        cells, tile, (level - start) * HALF + quarter, sign, rows,
                        speeds(base, level, quarter, sign, 1.0), from_x, from_y,
                    )
                    changes.append((tile, columns_in_order(sign), along, sides))
            old = [[out[t, column_of(ys[k]), :] for k in EDGE] for t, ys, _, _ in changes]
            for (t, ys, _, sides), before in zip(changes, old):
                for k, value, change in zip(EDGE, before, sides):
                    out[t, column_of(ys[k]), :] = value - change
            old = [[out[t, rows[k], :] for k in EDGE] for t, _, _, _ in changes]
            for (t, _, along, _), before in zip(changes, old):
                mine = t - start * TILES
                new = [value - change for value, change in zip(before, along)]
                for k, value in zip(EDGE, new):
                    out[t, rows[k], :] = value
                secondary[t] = new[0]
                primary[mine, 1] = new[2]
            for t, _, _, _ in changes:
                primary[t - start * TILES, 0] = out[t, rows[6], :]
            for quarter in range(group, group + GROUP):
                low = level * TILES + quarter
                send_y(out, (level - start) * HALF + quarter, low, low + HALF, across)
        return carry

    lax.fori_loop(start, stop, one, 0)


def finish_kernel(vel_size, levels, start, stop, partial, cells, from_x1, from_x2, from_y, *refs):
    from_y = halves(from_y)
    result, held, side, sems = refs[-4:]
    base = lax.axis_index("vel") * levels
    xs = order_of(flow_of(vel_size))
    rows = [row_of(x) for x in xs]
    width = TILES * LANES
    for sub in range(TILES):
        side[sub] = jnp.zeros((ROWS * ROWS, LANES), f32)

    def from_x(tile):
        here = tile - start * TILES
        return from_x1[here, 0], from_x1[here, 1], from_x2[tile]

    def copy(level):
        lanes = pl.ds(pl.multiple_of(level * width, width), width)
        here = level - start
        return pltpu.make_async_copy(held.at[here], result.at[:, :, lanes], sems.at[here])

    def one(level, carry):
        for quarter in range(HALF):
            for sign in (0, 1):
                sub = quarter + sign * HALF
                tile = level * TILES + sub
                ys = columns_in_order(sign)
                along, across = edge_changes(
                    cells, tile, (level - start) * HALF + quarter, sign, rows,
                    speeds(base, level, quarter, sign, 0.5), from_x, from_y,
                )
                for k, change in zip(EDGE, across):
                    side[sub, column_of(ys[k]), :] = change
                extra = dict(zip(EDGE, along))
                for k in range(ROWS):
                    new = partial[tile, rows[k], :] - side[sub, rows[k], :]
                    if k in extra:
                        new = new - extra[k]
                    held[level - start, xs[k], :, sub * LANES : (sub + 1) * LANES] = new
        copy(level).start()
        return carry

    lax.fori_loop(start, stop, one, 0)
    for level in range(start, stop):
        copy(level).wait()


def inner_kernel(vel_size, levels, start, stop, partial, cells, from_y, before, *refs):
    result, edges, held, side, sems = refs
    base = lax.axis_index("vel") * levels
    flow = flow_of(vel_size)
    xs = order_of(flow)
    rows = [row_of(x) for x in xs]
    first = jnp.where(flow, 2, 1)
    width = TILES * LANES
    from_y = halves(from_y)
    for sub in range(TILES):
        side[sub] = jnp.zeros((ROWS * ROWS, LANES), f32)

    def copy(level):
        lanes = pl.ds(pl.multiple_of(level * width, width), width)
        target = result.at[pl.ds(first, ROWS - len(EDGE)), :, lanes]
        return pltpu.make_async_copy(held.at[level - start], target, sems.at[level - start])

    def one(level, carry):
        for quarter in range(HALF):
            pair = (level - start) * HALF + quarter
            for sign in (0, 1):
                sub = quarter + sign * HALF
                tile = level * TILES + sub
                ys = columns_in_order(sign)
                speed = speeds(base, level, quarter, sign, 0.5)[1]
                changes = side_changes(cells, tile, pair, sign, speed, from_y)
                for k, change in zip(EDGE, changes):
                    side[sub, column_of(ys[k]), :] = change
                for k in range(ROWS):
                    new = partial[tile, rows[k], :] - side[sub, rows[k], :]
                    if k in EDGE:
                        edges[tile - start * TILES, EDGE.index(k)] = new
                    else:
                        lanes = slice(sub * LANES, (sub + 1) * LANES)
                        held[level - start, xs[k] - first, :, lanes] = new
        copy(level).start()
        return carry

    lax.fori_loop(start, stop, one, 0)
    for level in range(start, stop):
        copy(level).wait()


def edge_kernel(vel_size, levels, start, stop, edges, cells, from_x1, from_x2, before, *refs):
    result, pair, single, sems = refs
    base = lax.axis_index("vel") * levels
    flow = flow_of(vel_size)
    xs = order_of(flow)
    rows = [row_of(x) for x in xs]
    first = jnp.where(flow, 0, 6)
    width = TILES * LANES

    def from_x(tile):
        here = tile - start * TILES
        return from_x1[here, 0], from_x1[here, 1], from_x2[tile]

    def copies(level):
        lanes = pl.ds(pl.multiple_of(level * width, width), width)
        here = level - start
        double = result.at[pl.ds(first, 2), :, lanes]
        last = result.at[pl.ds(xs[ROWS - 1], 1), :, lanes]
        return (
            pltpu.make_async_copy(pair.at[here], double, sems.at[here, 0]),
            pltpu.make_async_copy(single.at[here], last, sems.at[here, 1]),
        )

    def one(level, carry):
        here = level - start
        speed = speeds(base, level, 0, 0, 0.5)[0]
        for sub in range(TILES):
            tile = level * TILES + sub
            lanes = slice(sub * LANES, (sub + 1) * LANES)
            changes = flow_changes(cells, tile, rows, speed, from_x)
            new = [edges[tile - start * TILES, i] - change for i, change in enumerate(changes)]
            pair[here, xs[0] - first, :, lanes] = new[0]
            pair[here, xs[1] - first, :, lanes] = new[1]
            single[here, 0, :, lanes] = new[2]
        for copy in copies(level):
            copy.start()
        return carry

    lax.fori_loop(start, stop, one, 0)
    for level in range(start, stop):
        for copy in copies(level):
            copy.wait()


def local(sizes, table):
    vel_size, sx_size, sy_size = sizes
    cells_x, cells_y, count = table.shape
    levels = count // (KV * KV)
    assert cells_x == ROWS and cells_y == ROWS and vel_size % 2 == 0
    assert count == levels * KV * KV
    first_part = levels * SPLIT[0] // SPLIT[1]
    bounds = [(0, first_part), (first_part, levels)] if 0 < first_part < levels else [(0, levels)]
    chunks = len(bounds)
    tiles = levels * TILES
    shape = lambda *dims: jax.ShapeDtypeStruct(dims, f32)
    cells_shape = shape(tiles, ROWS * ROWS, LANES)
    across_shape = [shape(2, (b - a) * HALF, 3, ROWS, LANES) for a, b in bounds]
    primary_shape = [shape((b - a) * TILES, 2, ROWS, LANES) for a, b in bounds]
    secondary_shape = shape(tiles, ROWS, LANES)
    whole = pl.BlockSpec(memory_space=pltpu.VMEM)
    outside = pl.BlockSpec(memory_space=pltpu.HBM)
    half = vel_size // 2

    def call(kernel, name, ins, outs, *args, scratch=(), aliases={}, static=()):
        specs = [outside if a.shape == table.shape else whole for a in args]
        return pl.pallas_call(
            functools.partial(kernel, *static),
            out_shape=outs,
            in_specs=specs,
            out_specs=ins,
            scratch_shapes=list(scratch),
            input_output_aliases=aliases,
            compiler_params=pltpu.CompilerParams(vmem_limit_bytes=16 * 1024 * 1024),
            name=name,
        )(*args)

    def along_x(array, sign):
        pairs = []
        for v in range(vel_size):
            way = sign if v >= half else -sign
            pairs += [(v * sx_size + i, v * sx_size + (i + way) % sx_size) for i in range(sx_size)]
        return lax.ppermute(array, ("vel", "sx"), pairs)

    def along_y(array):
        ways = [[(i, (i + way) % sy_size) for i in range(sy_size)] for way in (1, -1)]
        if sy_size == 2:
            return lax.ppermute(array, "sy", ways[0])
        return jnp.stack([lax.ppermute(array[i], "sy", ways[i]) for i in (0, 1)])

    def exchange(primary, secondary, across):
        behind = along_x(secondary, -1)
        return [(along_x(p, 1), behind, along_y(a)) for p, a in zip(primary, across)]

    def sums_of(cells):
        return call(sums_kernel, "sums", whole, shape(ROWS, LANES), cells, static=(levels,))

    def first_sums(sums):
        if vel_size > 4:
            return lax.psum(sums, "vel")
        return lax.all_gather(sums, "vel", axis=0, tiled=True)

    table_scratch = [
        pltpu.VMEM((ROWS, TILES, 3, ROWS, LANES), f32),
        pltpu.VMEM((ROWS, levels, 3, ROWS, LANES), f32),
        pltpu.VMEM((ROWS, ROWS, LANES), f32),
        pltpu.VMEM((2, ROWS * ROWS, LANES), f32),
    ]
    held = lambda count: pltpu.VMEM((count, ROWS, ROWS, TILES * LANES), f32)
    copies = lambda count: pltpu.SemaphoreType.DMA((count,))

    cells, *across, primary, secondary = call(
        pack_kernel, "pack", [whole] * (chunks + 3),
        [cells_shape] + across_shape + [primary_shape[0], secondary_shape],
        pltpu.with_memory_space_constraint(table, pltpu.HBM),
        scratch=[held(levels), copies(levels)], static=(vel_size, levels, bounds),
    )
    sums = first_sums(sums_of(cells))
    primary = [primary]
    for c in range(1, chunks):
        primary.append(
            call(
                late_kernel, "late", whole, primary_shape[c], cells, sums,
                static=(vel_size, *bounds[c]),
            )
        )
    arrived = exchange(primary, secondary, across)
    sectioned = call(
        local_kernel, "local", whole, cells_shape, cells, sums,
        scratch=table_scratch, static=(vel_size, levels, False),
    )
    primary, across, partly = [], [], ()
    for c, (begin, end) in enumerate(bounds):
        sectioned, first, secondary, last = call(
            correct_kernel, "correct", [whole] * 4,
            [cells_shape, primary_shape[c], secondary_shape, across_shape[c]],
            sectioned, cells, *arrived[c], *partly,
            static=(vel_size, levels, begin, end),
            aliases={0: 0, 5: 2} if partly else {0: 0},
        )
        partly = (secondary,)
        primary.append(first)
        across.append(last)
    arrived = exchange(primary, secondary, across)
    sums = first_sums(sums_of(sectioned))
    partial = call(
        local_kernel, "local", whole, cells_shape, sectioned, sums, cells,
        scratch=table_scratch, static=(vel_size, levels, True),
    )
    begin, end = bounds[0]
    result = call(
        finish_kernel, "finish", outside, shape(*table.shape), partial, sectioned, *arrived[0],
        scratch=[held(end), pltpu.VMEM((TILES, ROWS * ROWS, LANES), f32), copies(end)],
        static=(vel_size, levels, begin, end),
    )
    for c in range(1, chunks):
        begin, end = bounds[c]
        width = TILES * LANES
        result, edges = call(
            inner_kernel, "inner", [outside, whole],
            (shape(*table.shape), shape((end - begin) * TILES, len(EDGE), ROWS, LANES)),
            partial, sectioned, arrived[c][2], result,
            scratch=[
                pltpu.VMEM((end - begin, ROWS - len(EDGE), ROWS, width), f32),
                pltpu.VMEM((TILES, ROWS * ROWS, LANES), f32),
                copies(end - begin),
            ],
            static=(vel_size, levels, begin, end),
            aliases={3: 0},
        )
        result = call(
            edge_kernel, "edge", outside, shape(*table.shape),
            edges, sectioned, *arrived[c][:2], result,
            scratch=[
                pltpu.VMEM((end - begin, 2, ROWS, width), f32),
                pltpu.VMEM((end - begin, 1, ROWS, width), f32),
                pltpu.SemaphoreType.DMA((end - begin, 2)),
            ],
            static=(vel_size, levels, begin, end),
            aliases={4: 0},
        )
    return result


def solution(mesh):
    sizes = tuple(mesh.shape[name] for name in ("vel", "sx", "sy"))
    return jax.shard_map(
        functools.partial(local, sizes),
        mesh=mesh,
        in_specs=(P("sx", "sy", "vel"),),
        out_specs=P("sx", "sy", "vel"),
        check_vma=False,
    )
```

```python
import functools
import math

import jax
import jax.numpy as jnp
from jax import lax
from jax.experimental import pallas as pl
from jax.experimental.pallas import tpu as pltpu
from jax.sharding import PartitionSpec as P

KV = 32
SPLIT = (5, 8)
LANES = 128
ROWS = 8

vel_bound = 4.5
time_step = 0.25 / 4.5
collision_interval = 0.25
power_law_index = 0.81
diffusivity_ratio = 2.0 / 3.0
step = vel_bound / KV
weight = (2.0 * vel_bound / KV) ** 3 * (2.0 * math.pi) ** (-1.5)
f32 = jnp.float32

TILES = KV * KV // LANES
HALF = TILES // 2
PER_TILE = LANES // KV
SLOTS = LANES // ROWS


def limited(p, q):
    return jnp.maximum(jnp.minimum(p, jnp.maximum(q, 0.0)), jnp.minimum(q, 0.0))


def lane_index():
    return lax.broadcasted_iota(jnp.int32, (ROWS, LANES), 1)


def component(digit):
    return (2 * digit + 1 - KV).astype(f32) * step


def lane_components(tile):
    lane = lane_index()
    return component(tile * PER_TILE + lane // KV), component(lane % KV)


def flow_of(vel_size):
    return lax.axis_index("vel") >= vel_size // 2


def order_of(flow):
    return [jnp.where(flow, k, ROWS - 1 - k) for k in range(ROWS)]


def row_of(x):
    return pl.ds(pl.multiple_of(x * ROWS, ROWS), ROWS)


def column_of(y):
    return pl.ds(y, ROWS, stride=ROWS)


def lanes_of(tile):
    return pl.ds(pl.multiple_of(tile * LANES, LANES), LANES)


def columns_in_order(sign):
    return range(ROWS) if sign else range(ROWS - 1, -1, -1)


def inner_changes(cells):
    slopes = [cells[k + 1] - cells[k] for k in range(ROWS - 1)]
    faces = [cells[k] + 0.5 * limited(slopes[k - 1], slopes[k]) for k in range(1, ROWS - 1)]
    middle = [faces[k] - faces[k - 1] for k in range(1, ROWS - 2)]
    return [faces[0], *middle, -faces[-1]]


def outer_changes(far, near, p0, p1, p6, p7, ahead):
    slope = p0 - near
    entry = near + 0.5 * limited(near - far, slope)
    first = p0 + 0.5 * limited(slope, p1 - p0)
    leave = p7 + 0.5 * limited(p7 - p6, ahead - p7)
    return first - entry, -first, leave


def send_y(source, pair, low, high, across):
    across[0][pair, 0] = source[high, column_of(6), :]
    across[0][pair, 1] = source[high, column_of(7), :]
    across[0][pair, 2] = source[low, column_of(7), :]
    across[1][pair, 0] = source[low, column_of(1), :]
    across[1][pair, 1] = source[low, column_of(0), :]
    across[1][pair, 2] = source[high, column_of(0), :]


def pack_kernel(vel_size, levels, bounds, table, cells, *refs):
    chunks = len(bounds)
    across, primary, secondary = refs[:chunks], refs[chunks], refs[chunks + 1]
    held, sems = refs[-2], refs[-1]
    rows = [row_of(x) for x in order_of(flow_of(vel_size))]
    width = TILES * LANES

    def copy(level):
        lanes = pl.ds(pl.multiple_of(level * width, width), width)
        return pltpu.make_async_copy(table.at[:, :, lanes], held.at[level], sems.at[level])

    for level in range(levels):
        copy(level).start()
    for c, (begin, end) in enumerate(bounds):

        def one(level, carry, c=c, begin=begin):
            copy(level).wait()
            for quarter in range(HALF):
                low = level * TILES + quarter
                high = low + HALF
                for tile, sub in ((low, quarter), (high, quarter + HALF)):
                    for x in range(ROWS):
                        cells[tile, x * ROWS : (x + 1) * ROWS, :] = held[
                            level, x, :, sub * LANES : (sub + 1) * LANES
                        ]
                    if c == 0:
                        primary[tile, 0] = cells[tile, rows[6], :]
                        primary[tile, 1] = cells[tile, rows[7], :]
                    secondary[tile] = cells[tile, rows[0], :]
                send_y(cells, (level - begin) * HALF + quarter, low, high, halves(across[c]))
            return carry

        lax.fori_loop(begin, end, one, 0)


def late_kernel(vel_size, begin, end, cells, after, primary):
    rows = [row_of(x) for x in order_of(flow_of(vel_size))]

    def one(level, carry):
        for sub in range(TILES):
            tile = level * TILES + sub
            primary[tile - begin * TILES, 0] = cells[tile, rows[6], :]
            primary[tile - begin * TILES, 1] = cells[tile, rows[7], :]
        return carry

    lax.fori_loop(begin, end, one, 0)


def halves(across):
    return across.at[0], across.at[1]


def sums_kernel(levels, start, stop, cells, *refs):
    earlier, sums = refs[:-1], refs[-1]
    lane = lane_index()
    base = lax.axis_index("vel") * levels
    speed = {level: component(base + level) for level in range(start, stop)}

    def one(x, total):
        acc = [jnp.zeros((ROWS, LANES), f32) for _ in range(13)]
        row = row_of(x)
        for tile in range(TILES):
            cb, ce = lane_components(tile)
            m0 = m1 = m2 = m3 = None
            for level in range(start, stop):
                g = cells[level * TILES + tile, row, :]
                g1 = g * speed[level]
                g2 = g1 * speed[level]
                g3 = g2 * speed[level]
                if level == start:
                    m0, m1, m2, m3 = g, g1, g2, g3
                else:
                    m0, m1, m2, m3 = m0 + g, m1 + g1, m2 + g2, m3 + g3
            square = cb * cb + ce * ce
            b0 = cb * m0
            e0 = ce * m0
            terms = (
                m0, m1, b0, e0, m2, cb * b0, ce * e0, cb * m1, ce * m1, cb * e0,
                m3 + square * m1, cb * m2 + square * b0, ce * m2 + square * e0,
            )
            acc = [a + t for a, t in zip(acc, terms)]
        for m in range(13):
            total = jnp.where(lane == x * SLOTS + m, jnp.sum(acc[m], axis=1, keepdims=True), total)
        return total

    total = lax.fori_loop(0, ROWS, one, jnp.zeros((ROWS, LANES), f32))
    for part in earlier:
        total = total + part[...]
    sums[...] = total


def tables(parts, levels, base, scale, tab_b, tab_a, keep):
    sums = None
    for part in parts:
        for i in range(part.shape[0] // ROWS):
            more = part[i * ROWS : (i + 1) * ROWS, :]
            sums = more if sums is None else sums + more
    sums = sums * weight
    for x in range(ROWS):
        m = [
            jnp.broadcast_to(sums[:, x * SLOTS + i : x * SLOTS + i + 1], (ROWS, LANES))
            for i in range(13)
        ]
        n = m[0]
        inverse = 1.0 / n
        u = [m[i] * inverse for i in (1, 2, 3)]
        uu = u[0] * u[0] + u[1] * u[1] + u[2] * u[2]
        energy = m[4] + m[5] + m[6]
        temp = (energy * inverse - uu) * (1.0 / 3.0)
        rows = ((4, 7, 8), (7, 5, 9), (8, 9, 6))
        q = []
        for i in range(3):
            r = rows[i]
            stress = m[r[0]] * u[0] + m[r[1]] * u[1] + m[r[2]] * u[2]
            q.append(0.5 * (m[10 + i] - 2.0 * stress - u[i] * energy + 2.0 * n * u[i] * uu))
        log_temp = jnp.log(temp)
        rate = n * jnp.exp((1.0 - power_law_index) * log_temp) * (time_step / collision_interval)
        cold = 1.0 / temp
        half_cold = 0.5 * cold
        size = scale * rate * n * (cold * lax.rsqrt(temp))
        lift = (1.0 - diffusivity_ratio) / (5.0 * n * temp * temp)
        keep[x] = scale * (1.0 - rate)
        ql = [part * lift for part in q]
        for tile in range(TILES):
            cb, ce = lane_components(tile)
            db, de = cb - u[1], ce - u[2]
            square = db * db + de * de
            tab_b[x, tile, 0] = size * jnp.exp(-square * half_cold)
            tab_b[x, tile, 1] = db * ql[1] + de * ql[2]
            tab_b[x, tile, 2] = square * cold - 5.0
        for level in range(levels):
            da = component(base + level) - u[0]
            square = da * da
            tab_a[x, level, 0] = jnp.exp(-square * half_cold)
            tab_a[x, level, 1] = da * ql[0]
            tab_a[x, level, 2] = square * cold


def speeds(base, level, quarter, sign, scale):
    b_digit = quarter * PER_TILE + lane_index() // KV + sign * (KV // 2)
    a_speed = jnp.abs(component(base + level)) * (time_step * scale)
    return a_speed, jnp.abs(component(b_digit)) * (time_step * scale)


def local_kernel(vel_size, levels, last, *refs):
    cells, parts, first, (out, tab_b, tab_a, keep, side) = refs[0], refs[1:2], refs[2:-5], refs[-5:]
    scale = 0.5 if last else 1.0
    base = lax.axis_index("vel") * levels
    tables(parts, levels, base, scale, tab_b, tab_a, keep)
    xs = order_of(flow_of(vel_size))
    rows = [row_of(x) for x in xs]
    for sign in (0, 1):
        side[sign] = jnp.zeros((ROWS * ROWS, LANES), f32)

    def one(i, carry):
        level, quarter = i // HALF, i % HALF
        for sign in (0, 1):
            sub = quarter + sign * HALF
            tile = level * TILES + sub
            a_speed, b_speed = speeds(base, level, quarter, sign, scale)
            ys = columns_in_order(sign)
            line = [cells[tile, column_of(y), :] for y in ys]
            for k, change in enumerate(inner_changes(line)):
                side[sign, column_of(ys[k + 1]), :] = b_speed * change
            line = [cells[tile, row, :] for row in rows]
            changes = inner_changes(line)
            for k in range(ROWS):
                x, row = xs[k], rows[k]
                source = tab_a[x, level, 0] * tab_b[x, sub, 0]
                bend = tab_a[x, level, 1] + tab_b[x, sub, 1]
                wide = tab_a[x, level, 2] + tab_b[x, sub, 2]
                new = line[k] * keep[x] + (source + source * (bend * wide))
                moved = side[sign, row, :]
                if k > 0:
                    moved = moved + a_speed * changes[k - 1]
                new = new - moved
                if last:
                    new = 0.5 * first[0][tile, row, :] + new
                out[tile, row, :] = new
        return carry

    lax.fori_loop(0, levels * HALF, one, 0)


def side_changes(cells, tile, i, sign, speed, from_y):
    mine, other = 1 - sign, sign
    ys = columns_in_order(sign)
    line = [cells[tile, column_of(ys[k]), :] for k in (0, 1, 6, 7)]
    changes = outer_changes(from_y[mine][i, 0], from_y[mine][i, 1], *line, from_y[other][i, 2])
    return [speed * change for change in changes]


def flow_changes(cells, tile, rows, speed, from_x):
    line = [cells[tile, rows[k], :] for k in (0, 1, 6, 7)]
    far, near, ahead = from_x(tile)
    return [speed * change for change in outer_changes(far, near, *line, ahead)]


def edge_changes(cells, tile, i, sign, rows, speed, from_x, from_y):
    along = flow_changes(cells, tile, rows, speed[0], from_x)
    return along, side_changes(cells, tile, i, sign, speed[1], from_y)


EDGE = (0, 1, ROWS - 1)
GROUP = 1


def correct_kernel(vel_size, levels, start, stop, partial, cells, from_x1, from_x2, from_y, *refs):
    out, primary, secondary, across = refs[-4:]
    across, from_y = halves(across), halves(from_y)
    base = lax.axis_index("vel") * levels
    xs = order_of(flow_of(vel_size))
    rows = [row_of(x) for x in xs]

    def from_x(tile):
        here = tile - start * TILES
        return from_x1[here, 0], from_x1[here, 1], from_x2[tile]

    def one(level, carry):
        for group in range(0, HALF, GROUP):
            changes = []
            for quarter in range(group, group + GROUP):
                for sign in (0, 1):
                    tile = level * TILES + quarter + sign * HALF
                    along, sides = edge_changes(
                        cells, tile, (level - start) * HALF + quarter, sign, rows,
                        speeds(base, level, quarter, sign, 1.0), from_x, from_y,
                    )
                    changes.append((tile, columns_in_order(sign), along, sides))
            old = [[out[t, column_of(ys[k]), :] for k in EDGE] for t, ys, _, _ in changes]
            for (t, ys, _, sides), before in zip(changes, old):
                for k, value, change in zip(EDGE, before, sides):
                    out[t, column_of(ys[k]), :] = value - change
            old = [[out[t, rows[k], :] for k in EDGE] for t, _, _, _ in changes]
            for (t, _, along, _), before in zip(changes, old):
                mine = t - start * TILES
                new = [value - change for value, change in zip(before, along)]
                for k, value in zip(EDGE, new):
                    out[t, rows[k], :] = value
                secondary[t] = new[0]
                primary[mine, 1] = new[2]
            for t, _, _, _ in changes:
                primary[t - start * TILES, 0] = out[t, rows[6], :]
            for quarter in range(group, group + GROUP):
                low = level * TILES + quarter
                send_y(out, (level - start) * HALF + quarter, low, low + HALF, across)
        return carry

    lax.fori_loop(start, stop, one, 0)


def finish_kernel(vel_size, levels, start, stop, partial, cells, from_x1, from_x2, from_y, *refs):
    from_y = halves(from_y)
    result, held, side, sems = refs[-4:]
    base = lax.axis_index("vel") * levels
    xs = order_of(flow_of(vel_size))
    rows = [row_of(x) for x in xs]
    width = TILES * LANES
    for sub in range(TILES):
        side[sub] = jnp.zeros((ROWS * ROWS, LANES), f32)

    def from_x(tile):
        here = tile - start * TILES
        return from_x1[here, 0], from_x1[here, 1], from_x2[tile]

    def copy(level):
        lanes = pl.ds(pl.multiple_of(level * width, width), width)
        here = level - start
        return pltpu.make_async_copy(held.at[here], result.at[:, :, lanes], sems.at[here])

    def one(level, carry):
        for quarter in range(HALF):
            for sign in (0, 1):
                sub = quarter + sign * HALF
                tile = level * TILES + sub
                ys = columns_in_order(sign)
                along, across = edge_changes(
                    cells, tile, (level - start) * HALF + quarter, sign, rows,
                    speeds(base, level, quarter, sign, 0.5), from_x, from_y,
                )
                for k, change in zip(EDGE, across):
                    side[sub, column_of(ys[k]), :] = change
                extra = dict(zip(EDGE, along))
                for k in range(ROWS):
                    new = partial[tile, rows[k], :] - side[sub, rows[k], :]
                    if k in extra:
                        new = new - extra[k]
                    held[level - start, xs[k], :, sub * LANES : (sub + 1) * LANES] = new
        copy(level).start()
        return carry

    lax.fori_loop(start, stop, one, 0)
    for level in range(start, stop):
        copy(level).wait()


def inner_kernel(vel_size, levels, start, stop, partial, cells, from_y, before, *refs):
    result, edges, held, side, sems = refs
    base = lax.axis_index("vel") * levels
    flow = flow_of(vel_size)
    xs = order_of(flow)
    rows = [row_of(x) for x in xs]
    first = jnp.where(flow, 2, 1)
    width = TILES * LANES
    from_y = halves(from_y)
    for sub in range(TILES):
        side[sub] = jnp.zeros((ROWS * ROWS, LANES), f32)

    def copy(level):
        lanes = pl.ds(pl.multiple_of(level * width, width), width)
        target = result.at[pl.ds(first, ROWS - len(EDGE)), :, lanes]
        return pltpu.make_async_copy(held.at[level - start], target, sems.at[level - start])

    def one(level, carry):
        for quarter in range(HALF):
            pair = (level - start) * HALF + quarter
            for sign in (0, 1):
                sub = quarter + sign * HALF
                tile = level * TILES + sub
                ys = columns_in_order(sign)
                speed = speeds(base, level, quarter, sign, 0.5)[1]
                changes = side_changes(cells, tile, pair, sign, speed, from_y)
                for k, change in zip(EDGE, changes):
                    side[sub, column_of(ys[k]), :] = change
                for k in range(ROWS):
                    new = partial[tile, rows[k], :] - side[sub, rows[k], :]
                    if k in EDGE:
                        edges[tile - start * TILES, EDGE.index(k)] = new
                    else:
                        lanes = slice(sub * LANES, (sub + 1) * LANES)
                        held[level - start, xs[k] - first, :, lanes] = new
        copy(level).start()
        return carry

    lax.fori_loop(start, stop, one, 0)
    for level in range(start, stop):
        copy(level).wait()


def edge_kernel(vel_size, levels, start, stop, edges, cells, from_x1, from_x2, before, *refs):
    result, pair, single, sems = refs
    base = lax.axis_index("vel") * levels
    flow = flow_of(vel_size)
    xs = order_of(flow)
    rows = [row_of(x) for x in xs]
    first = jnp.where(flow, 0, 6)
    width = TILES * LANES

    def from_x(tile):
        here = tile - start * TILES
        return from_x1[here, 0], from_x1[here, 1], from_x2[tile]

    def copies(level):
        lanes = pl.ds(pl.multiple_of(level * width, width), width)
        here = level - start
        double = result.at[pl.ds(first, 2), :, lanes]
        last = result.at[pl.ds(xs[ROWS - 1], 1), :, lanes]
        return (
            pltpu.make_async_copy(pair.at[here], double, sems.at[here, 0]),
            pltpu.make_async_copy(single.at[here], last, sems.at[here, 1]),
        )

    def one(level, carry):
        here = level - start
        speed = speeds(base, level, 0, 0, 0.5)[0]
        for sub in range(TILES):
            tile = level * TILES + sub
            lanes = slice(sub * LANES, (sub + 1) * LANES)
            changes = flow_changes(cells, tile, rows, speed, from_x)
            new = [edges[tile - start * TILES, i] - change for i, change in enumerate(changes)]
            pair[here, xs[0] - first, :, lanes] = new[0]
            pair[here, xs[1] - first, :, lanes] = new[1]
            single[here, 0, :, lanes] = new[2]
        for copy in copies(level):
            copy.start()
        return carry

    lax.fori_loop(start, stop, one, 0)
    for level in range(start, stop):
        for copy in copies(level):
            copy.wait()


def local(sizes, table):
    vel_size, sx_size, sy_size = sizes
    cells_x, cells_y, count = table.shape
    levels = count // (KV * KV)
    assert cells_x == ROWS and cells_y == ROWS and vel_size % 2 == 0
    assert count == levels * KV * KV
    first_part = levels * SPLIT[0] // SPLIT[1]
    bounds = [(0, first_part), (first_part, levels)] if 0 < first_part < levels else [(0, levels)]
    chunks = len(bounds)
    tiles = levels * TILES
    shape = lambda *dims: jax.ShapeDtypeStruct(dims, f32)
    cells_shape = shape(tiles, ROWS * ROWS, LANES)
    across_shape = [shape(2, (b - a) * HALF, 3, ROWS, LANES) for a, b in bounds]
    primary_shape = [shape((b - a) * TILES, 2, ROWS, LANES) for a, b in bounds]
    secondary_shape = shape(tiles, ROWS, LANES)
    whole = pl.BlockSpec(memory_space=pltpu.VMEM)
    outside = pl.BlockSpec(memory_space=pltpu.HBM)
    half = vel_size // 2

    def call(kernel, name, ins, outs, *args, scratch=(), aliases={}, static=()):
        specs = [outside if a.shape == table.shape else whole for a in args]
        return pl.pallas_call(
            functools.partial(kernel, *static),
            out_shape=outs,
            in_specs=specs,
            out_specs=ins,
            scratch_shapes=list(scratch),
            input_output_aliases=aliases,
            compiler_params=pltpu.CompilerParams(vmem_limit_bytes=16 * 1024 * 1024),
            name=name,
        )(*args)

    def along_x(array, sign):
        pairs = []
        for v in range(vel_size):
            way = sign if v >= half else -sign
            pairs += [(v * sx_size + i, v * sx_size + (i + way) % sx_size) for i in range(sx_size)]
        return lax.ppermute(array, ("vel", "sx"), pairs)

    def along_y(array):
        ways = [[(i, (i + way) % sy_size) for i in range(sy_size)] for way in (1, -1)]
        if sy_size == 2:
            return lax.ppermute(array, "sy", ways[0])
        return jnp.stack([lax.ppermute(array[i], "sy", ways[i]) for i in (0, 1)])

    def exchange(primary, secondary, across):
        behind = along_x(secondary, -1)
        return [(along_x(p, 1), behind, along_y(a)) for p, a in zip(primary, across)]

    def sums_of(cells, begin=0, end=levels, *earlier):
        static = (levels, begin, end)
        return call(sums_kernel, "sums", whole, shape(ROWS, LANES), cells, *earlier, static=static)

    def first_sums(sums):
        if vel_size > 4:
            return lax.psum(sums, "vel")
        return lax.all_gather(sums, "vel", axis=0, tiled=True)

    table_scratch = [
        pltpu.VMEM((ROWS, TILES, 3, ROWS, LANES), f32),
        pltpu.VMEM((ROWS, levels, 3, ROWS, LANES), f32),
        pltpu.VMEM((ROWS, ROWS, LANES), f32),
        pltpu.VMEM((2, ROWS * ROWS, LANES), f32),
    ]
    held = lambda count: pltpu.VMEM((count, ROWS, ROWS, TILES * LANES), f32)
    copies = lambda count: pltpu.SemaphoreType.DMA((count,))

    cells, *across, primary, secondary = call(
        pack_kernel, "pack", [whole] * (chunks + 3),
        [cells_shape] + across_shape + [primary_shape[0], secondary_shape],
        pltpu.with_memory_space_constraint(table, pltpu.HBM),
        scratch=[held(levels), copies(levels)], static=(vel_size, levels, bounds),
    )
    sums = first_sums(sums_of(cells))
    primary = [primary]
    for c in range(1, chunks):
        primary.append(
            call(
                late_kernel, "late", whole, primary_shape[c], cells, sums,
                static=(vel_size, *bounds[c]),
            )
        )
    arrived = exchange(primary, secondary, across)
    sectioned = call(
        local_kernel, "local", whole, cells_shape, cells, sums,
        scratch=table_scratch, static=(vel_size, levels, False),
    )
    primary, across, partly, earlier = [], [], (), ()
    for c, (begin, end) in enumerate(bounds):
        sectioned, first, secondary, last = call(
            correct_kernel, "correct", [whole] * 4,
            [cells_shape, primary_shape[c], secondary_shape, across_shape[c]],
            sectioned, cells, *arrived[c], *partly, *earlier,
            static=(vel_size, levels, begin, end),
            aliases={0: 0, 5: 2} if partly else {0: 0},
        )
        partly = (secondary,)
        earlier = (sums_of(sectioned, begin, end, *earlier),)
        primary.append(first)
        across.append(last)
    arrived = exchange(primary, secondary, across)
    sums = first_sums(*earlier)
    partial = call(
        local_kernel, "local", whole, cells_shape, sectioned, sums, cells,
        scratch=table_scratch, static=(vel_size, levels, True),
    )
    begin, end = bounds[0]
    result = call(
        finish_kernel, "finish", outside, shape(*table.shape), partial, sectioned, *arrived[0],
        scratch=[held(end), pltpu.VMEM((TILES, ROWS * ROWS, LANES), f32), copies(end)],
        static=(vel_size, levels, begin, end),
    )
    for c in range(1, chunks):
        begin, end = bounds[c]
        width = TILES * LANES
        result, edges = call(
            inner_kernel, "inner", [outside, whole],
            (shape(*table.shape), shape((end - begin) * TILES, len(EDGE), ROWS, LANES)),
            partial, sectioned, arrived[c][2], result,
            scratch=[
                pltpu.VMEM((end - begin, ROWS - len(EDGE), ROWS, width), f32),
                pltpu.VMEM((TILES, ROWS * ROWS, LANES), f32),
                copies(end - begin),
            ],
            static=(vel_size, levels, begin, end),
            aliases={3: 0},
        )
        result = call(
            edge_kernel, "edge", outside, shape(*table.shape),
            edges, sectioned, *arrived[c][:2], result,
            scratch=[
                pltpu.VMEM((end - begin, 2, ROWS, width), f32),
                pltpu.VMEM((end - begin, 1, ROWS, width), f32),
                pltpu.SemaphoreType.DMA((end - begin, 2)),
            ],
            static=(vel_size, levels, begin, end),
            aliases={4: 0},
        )
    return result


def solution(mesh):
    sizes = tuple(mesh.shape[name] for name in ("vel", "sx", "sy"))
    return jax.shard_map(
        functools.partial(local, sizes),
        mesh=mesh,
        in_specs=(P("sx", "sy", "vel"),),
        out_specs=P("sx", "sy", "vel"),
        check_vma=False,
    )
```

```python
import functools
import math

import jax
import jax.numpy as jnp
from jax import lax
from jax.experimental import pallas as pl
from jax.experimental.pallas import tpu as pltpu
from jax.sharding import PartitionSpec as P

KV = 32
SPLIT = (5, 8)
LANES = 128
ROWS = 8

vel_bound = 4.5
time_step = 0.25 / 4.5
collision_interval = 0.25
power_law_index = 0.81
diffusivity_ratio = 2.0 / 3.0
step = vel_bound / KV
weight = (2.0 * vel_bound / KV) ** 3 * (2.0 * math.pi) ** (-1.5)
f32 = jnp.float32

TILES = KV * KV // LANES
HALF = TILES // 2
PER_TILE = LANES // KV
SLOTS = LANES // ROWS


def limited(p, q):
    return jnp.maximum(jnp.minimum(p, jnp.maximum(q, 0.0)), jnp.minimum(q, 0.0))


def lane_index():
    return lax.broadcasted_iota(jnp.int32, (ROWS, LANES), 1)


def component(digit):
    return (2 * digit + 1 - KV).astype(f32) * step


def lane_components(tile):
    lane = lane_index()
    return component(tile * PER_TILE + lane // KV), component(lane % KV)


def flow_of(vel_size):
    return lax.axis_index("vel") >= vel_size // 2


def order_of(flow):
    return [jnp.where(flow, k, ROWS - 1 - k) for k in range(ROWS)]


def row_of(x):
    return pl.ds(pl.multiple_of(x * ROWS, ROWS), ROWS)


def column_of(y):
    return pl.ds(y, ROWS, stride=ROWS)


def lanes_of(tile):
    return pl.ds(pl.multiple_of(tile * LANES, LANES), LANES)


def columns_in_order(sign):
    return range(ROWS) if sign else range(ROWS - 1, -1, -1)


def inner_changes(cells):
    slopes = [cells[k + 1] - cells[k] for k in range(ROWS - 1)]
    faces = [cells[k] + 0.5 * limited(slopes[k - 1], slopes[k]) for k in range(1, ROWS - 1)]
    middle = [faces[k] - faces[k - 1] for k in range(1, ROWS - 2)]
    return [faces[0], *middle, -faces[-1]]


def outer_changes(far, near, p0, p1, p6, p7, ahead):
    slope = p0 - near
    entry = near + 0.5 * limited(near - far, slope)
    first = p0 + 0.5 * limited(slope, p1 - p0)
    leave = p7 + 0.5 * limited(p7 - p6, ahead - p7)
    return first - entry, -first, leave


def send_y(source, pair, low, high, across):
    across[0][pair, 0] = source[high, column_of(6), :]
    across[0][pair, 1] = source[high, column_of(7), :]
    across[0][pair, 2] = source[low, column_of(7), :]
    across[1][pair, 0] = source[low, column_of(1), :]
    across[1][pair, 1] = source[low, column_of(0), :]
    across[1][pair, 2] = source[high, column_of(0), :]


def pack_kernel(vel_size, levels, bounds, table, cells, *refs):
    chunks = len(bounds)
    across, primary, secondary = refs[:chunks], refs[chunks], refs[chunks + 1]
    held, sems = refs[-2], refs[-1]
    xs = order_of(flow_of(vel_size))
    width = TILES * LANES

    def copy(level):
        lanes = pl.ds(pl.multiple_of(level * width, width), width)
        return pltpu.make_async_copy(table.at[:, :, lanes], held.at[level], sems.at[level])

    for level in range(levels):
        copy(level).start()
    for c, (begin, end) in enumerate(bounds):

        def one(level, carry, c=c, begin=begin):
            copy(level).wait()
            for quarter in range(HALF):
                low = level * TILES + quarter
                high = low + HALF
                for tile, sub in ((low, quarter), (high, quarter + HALF)):
                    for x in range(ROWS):
                        cells[tile, x * ROWS : (x + 1) * ROWS, :] = held[
                            level, x, :, sub * LANES : (sub + 1) * LANES
                        ]
                    if c == 0:
                        primary[tile, 0] = held[level, xs[6], :, sub * LANES : (sub + 1) * LANES]
                        primary[tile, 1] = held[level, xs[7], :, sub * LANES : (sub + 1) * LANES]
                    secondary[tile] = held[level, xs[0], :, sub * LANES : (sub + 1) * LANES]
                send_y(cells, (level - begin) * HALF + quarter, low, high, halves(across[c]))
            return carry

        lax.fori_loop(begin, end, one, 0)


def late_kernel(vel_size, begin, end, cells, after, primary):
    rows = [row_of(x) for x in order_of(flow_of(vel_size))]

    def one(level, carry):
        for sub in range(TILES):
            tile = level * TILES + sub
            primary[tile - begin * TILES, 0] = cells[tile, rows[6], :]
            primary[tile - begin * TILES, 1] = cells[tile, rows[7], :]
        return carry

    lax.fori_loop(begin, end, one, 0)


def halves(across):
    return across.at[0], across.at[1]


def sums_kernel(levels, start, stop, cells, *refs):
    earlier, sums = refs[:-1], refs[-1]
    lane = lane_index()
    base = lax.axis_index("vel") * levels
    speed = {level: component(base + level) for level in range(start, stop)}

    def one(x, total):
        acc = [jnp.zeros((ROWS, LANES), f32) for _ in range(13)]
        row = row_of(x)
        for tile in range(TILES):
            cb, ce = lane_components(tile)
            m0 = m1 = m2 = m3 = None
            for level in range(start, stop):
                g = cells[level * TILES + tile, row, :]
                g1 = g * speed[level]
                g2 = g1 * speed[level]
                g3 = g2 * speed[level]
                if level == start:
                    m0, m1, m2, m3 = g, g1, g2, g3
                else:
                    m0, m1, m2, m3 = m0 + g, m1 + g1, m2 + g2, m3 + g3
            square = cb * cb + ce * ce
            b0 = cb * m0
            e0 = ce * m0
            terms = (
                m0, m1, b0, e0, m2, cb * b0, ce * e0, cb * m1, ce * m1, cb * e0,
                m3 + square * m1, cb * m2 + square * b0, ce * m2 + square * e0,
            )
            acc = [a + t for a, t in zip(acc, terms)]
        for m in range(13):
            total = jnp.where(lane == x * SLOTS + m, jnp.sum(acc[m], axis=1, keepdims=True), total)
        return total

    total = lax.fori_loop(0, ROWS, one, jnp.zeros((ROWS, LANES), f32))
    for part in earlier:
        total = total + part[...]
    sums[...] = total


def tables(parts, levels, base, scale, tab_b, tab_a, keep):
    sums = None
    for part in parts:
        for i in range(part.shape[0] // ROWS):
            more = part[i * ROWS : (i + 1) * ROWS, :]
            sums = more if sums is None else sums + more
    sums = sums * weight
    for x in range(ROWS):
        m = [
            jnp.broadcast_to(sums[:, x * SLOTS + i : x * SLOTS + i + 1], (ROWS, LANES))
            for i in range(13)
        ]
        n = m[0]
        inverse = 1.0 / n
        u = [m[i] * inverse for i in (1, 2, 3)]
        uu = u[0] * u[0] + u[1] * u[1] + u[2] * u[2]
        energy = m[4] + m[5] + m[6]
        temp = (energy * inverse - uu) * (1.0 / 3.0)
        rows = ((4, 7, 8), (7, 5, 9), (8, 9, 6))
        q = []
        for i in range(3):
            r = rows[i]
            stress = m[r[0]] * u[0] + m[r[1]] * u[1] + m[r[2]] * u[2]
            q.append(0.5 * (m[10 + i] - 2.0 * stress - u[i] * energy + 2.0 * n * u[i] * uu))
        log_temp = jnp.log(temp)
        rate = n * jnp.exp((1.0 - power_law_index) * log_temp) * (time_step / collision_interval)
        cold = 1.0 / temp
        half_cold = 0.5 * cold
        size = scale * rate * n * (cold * lax.rsqrt(temp))
        lift = (1.0 - diffusivity_ratio) / (5.0 * n * temp * temp)
        keep[x] = scale * (1.0 - rate)
        ql = [part * lift for part in q]
        for tile in range(TILES):
            cb, ce = lane_components(tile)
            db, de = cb - u[1], ce - u[2]
            square = db * db + de * de
            tab_b[x, tile, 0] = size * jnp.exp(-square * half_cold)
            tab_b[x, tile, 1] = db * ql[1] + de * ql[2]
            tab_b[x, tile, 2] = square * cold - 5.0
        for level in range(levels):
            da = component(base + level) - u[0]
            square = da * da
            tab_a[x, level, 0] = jnp.exp(-square * half_cold)
            tab_a[x, level, 1] = da * ql[0]
            tab_a[x, level, 2] = square * cold


def speeds(base, level, quarter, sign, scale):
    b_digit = quarter * PER_TILE + lane_index() // KV + sign * (KV // 2)
    a_speed = jnp.abs(component(base + level)) * (time_step * scale)
    return a_speed, jnp.abs(component(b_digit)) * (time_step * scale)


def local_kernel(vel_size, levels, last, *refs):
    cells, parts, first, (out, tab_b, tab_a, keep, side) = refs[0], refs[1:2], refs[2:-5], refs[-5:]
    scale = 0.5 if last else 1.0
    base = lax.axis_index("vel") * levels
    tables(parts, levels, base, scale, tab_b, tab_a, keep)
    xs = order_of(flow_of(vel_size))
    rows = [row_of(x) for x in xs]
    for sign in (0, 1):
        side[sign] = jnp.zeros((ROWS * ROWS, LANES), f32)

    def one(i, carry):
        level, quarter = i // HALF, i % HALF
        for sign in (0, 1):
            sub = quarter + sign * HALF
            tile = level * TILES + sub
            a_speed, b_speed = speeds(base, level, quarter, sign, scale)
            ys = columns_in_order(sign)
            line = [cells[tile, column_of(y), :] for y in ys]
            for k, change in enumerate(inner_changes(line)):
                side[sign, column_of(ys[k + 1]), :] = b_speed * change
            line = [cells[tile, row, :] for row in rows]
            changes = inner_changes(line)
            for k in range(ROWS):
                x, row = xs[k], rows[k]
                source = tab_a[x, level, 0] * tab_b[x, sub, 0]
                bend = tab_a[x, level, 1] + tab_b[x, sub, 1]
                wide = tab_a[x, level, 2] + tab_b[x, sub, 2]
                new = line[k] * keep[x] + (source + source * (bend * wide))
                moved = side[sign, row, :]
                if k > 0:
                    moved = moved + a_speed * changes[k - 1]
                new = new - moved
                if last:
                    new = 0.5 * first[0][tile, row, :] + new
                out[tile, row, :] = new
        return carry

    lax.fori_loop(0, levels * HALF, one, 0)


def side_changes(cells, tile, i, sign, speed, from_y):
    mine, other = 1 - sign, sign
    ys = columns_in_order(sign)
    line = [cells[tile, column_of(ys[k]), :] for k in (0, 1, 6, 7)]
    changes = outer_changes(from_y[mine][i, 0], from_y[mine][i, 1], *line, from_y[other][i, 2])
    return [speed * change for change in changes]


def flow_changes(cells, tile, rows, speed, from_x):
    line = [cells[tile, rows[k], :] for k in (0, 1, 6, 7)]
    far, near, ahead = from_x(tile)
    return [speed * change for change in outer_changes(far, near, *line, ahead)]


def edge_changes(cells, tile, i, sign, rows, speed, from_x, from_y):
    along = flow_changes(cells, tile, rows, speed[0], from_x)
    return along, side_changes(cells, tile, i, sign, speed[1], from_y)


EDGE = (0, 1, ROWS - 1)
GROUP = 1


def correct_kernel(vel_size, levels, start, stop, partial, cells, from_x1, from_x2, from_y, *refs):
    out, primary, secondary, across = refs[-4:]
    across, from_y = halves(across), halves(from_y)
    base = lax.axis_index("vel") * levels
    xs = order_of(flow_of(vel_size))
    rows = [row_of(x) for x in xs]

    def from_x(tile):
        here = tile - start * TILES
        return from_x1[here, 0], from_x1[here, 1], from_x2[tile]

    def one(level, carry):
        for group in range(0, HALF, GROUP):
            changes = []
            for quarter in range(group, group + GROUP):
                for sign in (0, 1):
                    tile = level * TILES + quarter + sign * HALF
                    along, sides = edge_changes(
                        cells, tile, (level - start) * HALF + quarter, sign, rows,
                        speeds(base, level, quarter, sign, 1.0), from_x, from_y,
                    )
                    changes.append((tile, columns_in_order(sign), along, sides))
            old = [[out[t, column_of(ys[k]), :] for k in EDGE] for t, ys, _, _ in changes]
            for (t, ys, _, sides), before in zip(changes, old):
                for k, value, change in zip(EDGE, before, sides):
                    out[t, column_of(ys[k]), :] = value - change
            old = [[out[t, rows[k], :] for k in EDGE] for t, _, _, _ in changes]
            for (t, _, along, _), before in zip(changes, old):
                mine = t - start * TILES
                new = [value - change for value, change in zip(before, along)]
                for k, value in zip(EDGE, new):
                    out[t, rows[k], :] = value
                secondary[t] = new[0]
                primary[mine, 1] = new[2]
            for t, _, _, _ in changes:
                primary[t - start * TILES, 0] = out[t, rows[6], :]
            for quarter in range(group, group + GROUP):
                low = level * TILES + quarter
                send_y(out, (level - start) * HALF + quarter, low, low + HALF, across)
        return carry

    lax.fori_loop(start, stop, one, 0)


def finish_kernel(vel_size, levels, start, stop, partial, cells, from_x1, from_x2, from_y, *refs):
    from_y = halves(from_y)
    result, held, side, sems = refs[-4:]
    base = lax.axis_index("vel") * levels
    xs = order_of(flow_of(vel_size))
    rows = [row_of(x) for x in xs]
    width = TILES * LANES
    for sub in range(TILES):
        side[sub] = jnp.zeros((ROWS * ROWS, LANES), f32)

    def from_x(tile):
        here = tile - start * TILES
        return from_x1[here, 0], from_x1[here, 1], from_x2[tile]

    def copy(level):
        lanes = pl.ds(pl.multiple_of(level * width, width), width)
        here = level - start
        return pltpu.make_async_copy(held.at[here], result.at[:, :, lanes], sems.at[here])

    def one(level, carry):
        for quarter in range(HALF):
            for sign in (0, 1):
                sub = quarter + sign * HALF
                tile = level * TILES + sub
                ys = columns_in_order(sign)
                along, across = edge_changes(
                    cells, tile, (level - start) * HALF + quarter, sign, rows,
                    speeds(base, level, quarter, sign, 0.5), from_x, from_y,
                )
                for k, change in zip(EDGE, across):
                    side[sub, column_of(ys[k]), :] = change
                extra = dict(zip(EDGE, along))
                for k in range(ROWS):
                    new = partial[tile, rows[k], :] - side[sub, rows[k], :]
                    if k in extra:
                        new = new - extra[k]
                    held[level - start, xs[k], :, sub * LANES : (sub + 1) * LANES] = new
        copy(level).start()
        return carry

    lax.fori_loop(start, stop, one, 0)
    for level in range(start, stop):
        copy(level).wait()


def inner_kernel(vel_size, levels, start, stop, partial, cells, from_y, before, *refs):
    result, edges, held, side, sems = refs
    base = lax.axis_index("vel") * levels
    flow = flow_of(vel_size)
    xs = order_of(flow)
    rows = [row_of(x) for x in xs]
    first = jnp.where(flow, 2, 1)
    width = TILES * LANES
    from_y = halves(from_y)
    for sub in range(TILES):
        side[sub] = jnp.zeros((ROWS * ROWS, LANES), f32)

    def copy(level):
        lanes = pl.ds(pl.multiple_of(level * width, width), width)
        target = result.at[pl.ds(first, ROWS - len(EDGE)), :, lanes]
        return pltpu.make_async_copy(held.at[level - start], target, sems.at[level - start])

    def one(level, carry):
        for quarter in range(HALF):
            pair = (level - start) * HALF + quarter
            for sign in (0, 1):
                sub = quarter + sign * HALF
                tile = level * TILES + sub
                ys = columns_in_order(sign)
                speed = speeds(base, level, quarter, sign, 0.5)[1]
                changes = side_changes(cells, tile, pair, sign, speed, from_y)
                for k, change in zip(EDGE, changes):
                    side[sub, column_of(ys[k]), :] = change
                for k in range(ROWS):
                    new = partial[tile, rows[k], :] - side[sub, rows[k], :]
                    if k in EDGE:
                        edges[tile - start * TILES, EDGE.index(k)] = new
                    else:
                        lanes = slice(sub * LANES, (sub + 1) * LANES)
                        held[level - start, xs[k] - first, :, lanes] = new
        copy(level).start()
        return carry

    lax.fori_loop(start, stop, one, 0)
    for level in range(start, stop):
        copy(level).wait()


def edge_kernel(vel_size, levels, start, stop, edges, cells, from_x1, from_x2, before, *refs):
    result, pair, single, sems = refs
    base = lax.axis_index("vel") * levels
    flow = flow_of(vel_size)
    xs = order_of(flow)
    rows = [row_of(x) for x in xs]
    first = jnp.where(flow, 0, 6)
    width = TILES * LANES

    def from_x(tile):
        here = tile - start * TILES
        return from_x1[here, 0], from_x1[here, 1], from_x2[tile]

    def copies(level):
        lanes = pl.ds(pl.multiple_of(level * width, width), width)
        here = level - start
        double = result.at[pl.ds(first, 2), :, lanes]
        last = result.at[pl.ds(xs[ROWS - 1], 1), :, lanes]
        return (
            pltpu.make_async_copy(pair.at[here], double, sems.at[here, 0]),
            pltpu.make_async_copy(single.at[here], last, sems.at[here, 1]),
        )

    def one(level, carry):
        here = level - start
        speed = speeds(base, level, 0, 0, 0.5)[0]
        for sub in range(TILES):
            tile = level * TILES + sub
            lanes = slice(sub * LANES, (sub + 1) * LANES)
            changes = flow_changes(cells, tile, rows, speed, from_x)
            new = [edges[tile - start * TILES, i] - change for i, change in enumerate(changes)]
            pair[here, xs[0] - first, :, lanes] = new[0]
            pair[here, xs[1] - first, :, lanes] = new[1]
            single[here, 0, :, lanes] = new[2]
        for copy in copies(level):
            copy.start()
        return carry

    lax.fori_loop(start, stop, one, 0)
    for level in range(start, stop):
        for copy in copies(level):
            copy.wait()


def local(sizes, table):
    vel_size, sx_size, sy_size = sizes
    cells_x, cells_y, count = table.shape
    levels = count // (KV * KV)
    assert cells_x == ROWS and cells_y == ROWS and vel_size % 2 == 0
    assert count == levels * KV * KV
    first_part = levels * SPLIT[0] // SPLIT[1]
    bounds = [(0, first_part), (first_part, levels)] if 0 < first_part < levels else [(0, levels)]
    chunks = len(bounds)
    tiles = levels * TILES
    shape = lambda *dims: jax.ShapeDtypeStruct(dims, f32)
    cells_shape = shape(tiles, ROWS * ROWS, LANES)
    across_shape = [shape(2, (b - a) * HALF, 3, ROWS, LANES) for a, b in bounds]
    primary_shape = [shape((b - a) * TILES, 2, ROWS, LANES) for a, b in bounds]
    secondary_shape = shape(tiles, ROWS, LANES)
    whole = pl.BlockSpec(memory_space=pltpu.VMEM)
    outside = pl.BlockSpec(memory_space=pltpu.HBM)
    half = vel_size // 2

    def call(kernel, name, ins, outs, *args, scratch=(), aliases={}, static=()):
        specs = [outside if a.shape == table.shape else whole for a in args]
        return pl.pallas_call(
            functools.partial(kernel, *static),
            out_shape=outs,
            in_specs=specs,
            out_specs=ins,
            scratch_shapes=list(scratch),
            input_output_aliases=aliases,
            compiler_params=pltpu.CompilerParams(vmem_limit_bytes=16 * 1024 * 1024),
            name=name,
        )(*args)

    def along_x(array, sign):
        pairs = []
        for v in range(vel_size):
            way = sign if v >= half else -sign
            pairs += [(v * sx_size + i, v * sx_size + (i + way) % sx_size) for i in range(sx_size)]
        return lax.ppermute(array, ("vel", "sx"), pairs)

    def along_y(array):
        ways = [[(i, (i + way) % sy_size) for i in range(sy_size)] for way in (1, -1)]
        if sy_size == 2:
            return lax.ppermute(array, "sy", ways[0])
        return jnp.stack([lax.ppermute(array[i], "sy", ways[i]) for i in (0, 1)])

    def exchange(primary, secondary, across):
        behind = along_x(secondary, -1)
        return [(along_x(p, 1), behind, along_y(a)) for p, a in zip(primary, across)]

    def sums_of(cells, begin=0, end=levels, *earlier):
        static = (levels, begin, end)
        return call(sums_kernel, "sums", whole, shape(ROWS, LANES), cells, *earlier, static=static)

    def first_sums(sums):
        if vel_size > 4:
            return lax.psum(sums, "vel")
        return lax.all_gather(sums, "vel", axis=0, tiled=True)

    table_scratch = [
        pltpu.VMEM((ROWS, TILES, 3, ROWS, LANES), f32),
        pltpu.VMEM((ROWS, levels, 3, ROWS, LANES), f32),
        pltpu.VMEM((ROWS, ROWS, LANES), f32),
        pltpu.VMEM((2, ROWS * ROWS, LANES), f32),
    ]
    held = lambda count: pltpu.VMEM((count, ROWS, ROWS, TILES * LANES), f32)
    copies = lambda count: pltpu.SemaphoreType.DMA((count,))

    cells, *across, primary, secondary = call(
        pack_kernel, "pack", [whole] * (chunks + 3),
        [cells_shape] + across_shape + [primary_shape[0], secondary_shape],
        pltpu.with_memory_space_constraint(table, pltpu.HBM),
        scratch=[held(levels), copies(levels)], static=(vel_size, levels, bounds),
    )
    sums = first_sums(sums_of(cells))
    primary = [primary]
    for c in range(1, chunks):
        primary.append(
            call(
                late_kernel, "late", whole, primary_shape[c], cells, sums,
                static=(vel_size, *bounds[c]),
            )
        )
    arrived = exchange(primary, secondary, across)
    sectioned = call(
        local_kernel, "local", whole, cells_shape, cells, sums,
        scratch=table_scratch, static=(vel_size, levels, False),
    )
    primary, across, partly, earlier = [], [], (), ()
    for c, (begin, end) in enumerate(bounds):
        sectioned, first, secondary, last = call(
            correct_kernel, "correct", [whole] * 4,
            [cells_shape, primary_shape[c], secondary_shape, across_shape[c]],
            sectioned, cells, *arrived[c], *partly, *earlier,
            static=(vel_size, levels, begin, end),
            aliases={0: 0, 5: 2} if partly else {0: 0},
        )
        partly = (secondary,)
        earlier = (sums_of(sectioned, begin, end, *earlier),)
        primary.append(first)
        across.append(last)
    arrived = exchange(primary, secondary, across)
    sums = first_sums(*earlier)
    partial = call(
        local_kernel, "local", whole, cells_shape, sectioned, sums, cells,
        scratch=table_scratch, static=(vel_size, levels, True),
    )
    begin, end = bounds[0]
    result = call(
        finish_kernel, "finish", outside, shape(*table.shape), partial, sectioned, *arrived[0],
        scratch=[held(end), pltpu.VMEM((TILES, ROWS * ROWS, LANES), f32), copies(end)],
        static=(vel_size, levels, begin, end),
    )
    for c in range(1, chunks):
        begin, end = bounds[c]
        width = TILES * LANES
        result, edges = call(
            inner_kernel, "inner", [outside, whole],
            (shape(*table.shape), shape((end - begin) * TILES, len(EDGE), ROWS, LANES)),
            partial, sectioned, arrived[c][2], result,
            scratch=[
                pltpu.VMEM((end - begin, ROWS - len(EDGE), ROWS, width), f32),
                pltpu.VMEM((TILES, ROWS * ROWS, LANES), f32),
                copies(end - begin),
            ],
            static=(vel_size, levels, begin, end),
            aliases={3: 0},
        )
        result = call(
            edge_kernel, "edge", outside, shape(*table.shape),
            edges, sectioned, *arrived[c][:2], result,
            scratch=[
                pltpu.VMEM((end - begin, 2, ROWS, width), f32),
                pltpu.VMEM((end - begin, 1, ROWS, width), f32),
                pltpu.SemaphoreType.DMA((end - begin, 2)),
            ],
            static=(vel_size, levels, begin, end),
            aliases={4: 0},
        )
    return result


def solution(mesh):
    sizes = tuple(mesh.shape[name] for name in ("vel", "sx", "sy"))
    return jax.shard_map(
        functools.partial(local, sizes),
        mesh=mesh,
        in_specs=(P("sx", "sy", "vel"),),
        out_specs=P("sx", "sy", "vel"),
        check_vma=False,
    )
```
